256 devices in a mesh: span: 64 (over x, z, core), space: 4 (over y).
Axes of the slice: x: 4, y: 4, z: 8, core: 2. Of those that a mesh axis runs over, the one named last changes fastest.
Arguments:
- frames: bfloat16 [64, 4, 8, 128, 128], P('span', None, 'space'), may hold values from -200 to 200
- cotangent: bfloat16 [64, 4, 8, 128, 128], P('span', None, 'space'), may hold values from -6 to 6
- conv_weight: bfloat16 [3, 3, 3, 128, 128], replicated, may hold values from -0.109375 to 0.109375
- conv_bias: float32 [128], replicated, may hold values from -3 to 3
- norm_gain: float32 [128], replicated, may hold values from 0.1 to 1.9
- norm_shift: float32 [128], replicated, may hold values from -3 to 3
- clip_ids: int32 [64], replicated, may hold values from 0 to 8, never falling along the last dimension, each value on 1 to 32 neighbouring positions
Outputs:
- encoded: bfloat16 [64, 4, 8, 128, 128], P('span', None, 'space')
- frames_grad: bfloat16 [64, 4, 8, 128, 128], P('span', None, 'space')
- weight_grad: float32 [3, 3, 3, 128, 128], replicated
- bias_grad: float32 [128], replicated
- gain_grad: float32 [128], replicated
- shift_grad: float32 [128], replicated
The draws below stay inside these ranges and needn't reach their ends.
Inputs may be any that keep to these rules, and one draw needn't show every extreme that they name: `clip_ids`: clip numbers never fall along the spans; every clip 0 to 8 holds 1 to 32 consecutive spans, one of them exactly 32.
All inputs are finite; a program needn't handle non-finite values.
Results may differ from the reference program's by a relative error of at most 0.0042.
Values may be sent and summed in bfloat16 or wider, within the bound.
A program may use at most 64 MiB of HBM per device.

```python
import math
import jax
import jax.numpy as jnp
import numpy as np
from jax import lax

C = 128
GROUPS = 32
FR = 4
WC = 128
SPANS = 64
ROWS = 8
NCLIP = 9
MOST = 32
POSITIONS = 262144


def draw_frames(key, part):
    key = jax.random.fold_in(key, 11)
    key_base, key_channel, key_frame, key_offset = jax.random.split(key, 4)
    full_shape = (SPANS, FR, ROWS, WC, C)
    ramp_position = jnp.arange(SPANS, dtype=jnp.float32) / max(SPANS - 1, 1)
    channel_scale = jnp.exp(jax.random.uniform(key_channel, (C,), minval=0.0, maxval=math.log(10.0)))
    frame_scale = jax.random.uniform(key_frame, (SPANS, FR, 1, 1, 1), minval=0.6, maxval=1.6)
    base_values = jax.random.normal(key_base, full_shape)
    span_scale = 3.0 ** ramp_position
    offset = 0.3 * jax.random.normal(key_offset, (1, 1, 1, 1, C))
    values = (base_values + offset) * channel_scale * span_scale[:, None, None, None, None] * frame_scale
    return jnp.clip(values, -200.0, 200.0).astype(jnp.bfloat16)


def levels(key, shape, cuts, low, largest):
    loudness = 1.0
    for axis_at, shards_of in cuts:
        heights = jax.random.uniform(jax.random.fold_in(jax.random.fold_in(key, 6), axis_at), (shards_of,), jnp.float32, low / len(cuts), largest / len(cuts))
        loudness = loudness * jnp.repeat(jnp.exp(heights), shape[axis_at] // shards_of).reshape((-1,) + (1,) * (len(shape) - 1 - axis_at))
    return loudness


def profile(amount, total, bound, skew):
    loads = [(1 << 20) // math.isqrt(rank ** skew) + 1 for rank in range(2, amount + 1)]
    spare, holding = total - bound - (amount - 1), [1] * (amount - 1)
    while spare > 0:
        free = [i for i in range(amount - 1) if holding[i] < bound]
        pool, remaining = sum([loads[i] for i in free]), spare
        for i in free:
            addition = min(bound - holding[i], max(1, remaining * loads[i] // pool), spare)
            holding[i] = holding[i] + addition
            spare = spare - addition
    return np.array([bound] + holding)


def uneven_parts(own_key, count, total, limit, skew):
    if count == 2:
        one = jax.random.randint(own_key, (), max(1, total - limit), min(limit, total - 1) + 1)
        return jnp.stack([one, total - one])
    tallies = jnp.asarray(profile(count, total, limit, skew), jnp.int32)
    couples = (count - 1) // 2
    source_of, receiver = tallies[1:1 + 2 * couples:2], tallies[2:2 + 2 * couples:2]
    slack = jnp.minimum(source_of - 1, limit - receiver)
    moved = jax.random.randint(jax.random.fold_in(own_key, 1), (couples,), 0, 1 << 20) % (slack + 1)
    tallies = tallies.at[1:1 + 2 * couples:2].set(source_of - moved).at[2:2 + 2 * couples:2].set(receiver + moved)
    return tallies[jax.random.permutation(jax.random.fold_in(own_key, 2), count)]


def normal_values(rng, shape, width, limit, cuts=(), kind=jnp.bfloat16):
    drawn = jax.random.normal(rng, shape, jnp.float32) * width
    if len(cuts) > 0:
        drawn = levels(rng, shape, cuts, -0.22, 0.18) * drawn
    return jnp.clip(drawn, min=-limit, max=limit).astype(kind)


def setup_inputs(seed: int = 0) -> dict:
    splits = jax.random.split(jax.random.key(seed), 8)
    frames = draw_frames(jax.random.fold_in(splits[7], 71), 0)
    cotangent = normal_values(splits[1], (SPANS, FR, ROWS, WC, C), 1.0, 6.0, ((0, 64), (2, 4)))
    conv_weight = normal_values(splits[2], (3, 3, 3, C, C), (27 * C) ** -0.5, 0.109375)
    conv_bias = normal_values(splits[3], (C,), 0.5, 3.0, (), jnp.float32)
    norm_gain = jnp.clip(1.0 + 0.18 * jax.random.normal(splits[4], (C,), jnp.float32), 0.1, 1.9)
    norm_shift = normal_values(splits[5], (C,), 0.5, 3.0, (), jnp.float32)
    clip_ids = jnp.searchsorted(jnp.cumsum(uneven_parts(splits[6], NCLIP, SPANS, MOST, 2)), jnp.arange(SPANS), side="right").astype(jnp.int32)
    return dict(frames=frames, cotangent=cotangent, conv_weight=conv_weight, conv_bias=conv_bias, norm_gain=norm_gain, norm_shift=norm_shift, clip_ids=clip_ids)


epsilon = 1e-06

def conv_block(padded, kernel):
    frame_count = padded.shape[0] - 2
    row_count = padded.shape[1] - 2
    col_count = padded.shape[2] - 2
    channels = padded.shape[3]
    stacked = jnp.concatenate([padded[:, :, col_tap:col_tap + col_count] for col_tap in range(3)], axis=-1)
    summed = jnp.zeros((frame_count * row_count * col_count, kernel.shape[-1]), jnp.float32)
    for time_tap in range(3):
        for row_tap in range(3):
            window = stacked[time_tap:time_tap + frame_count, row_tap:row_tap + row_count]
            window = window.reshape(frame_count * row_count * col_count, 3 * channels)
            summed = summed + jnp.dot(window, kernel[time_tap, row_tap], preferred_element_type=jnp.float32)
    return summed.reshape(frame_count, row_count, col_count, kernel.shape[-1])

def weight_block(padded, cot_block):
    frame_count, row_count, col_count, channels = cot_block.shape
    stacked = jnp.concatenate([padded[:, :, col_tap:col_tap + col_count] for col_tap in range(3)], axis=-1)
    flat_cot = cot_block.reshape(-1, channels)
    pieces = []
    for time_tap in range(3):
        for row_tap in range(3):
            window = stacked[time_tap:time_tap + frame_count, row_tap:row_tap + row_count]
            window = window.reshape(-1, stacked.shape[-1])
            pieces.append(lax.dot_general(window, flat_cot, (((0,), (0,)), ((), ())), preferred_element_type=jnp.float32))
    return jnp.stack(pieces).reshape(3, 3, 3, stacked.shape[-1] // 3, channels)

def normalize(frame_block, center, inv_scale, norm_gain, norm_shift):
    channels = frame_block.shape[-1]
    grouped = frame_block.astype(jnp.float32).reshape(-1, GROUPS, channels // GROUPS)
    normed = ((grouped - center[None, :, None]) * inv_scale[None, :, None]).reshape(frame_block.shape)
    return (normed, normed * norm_gain + norm_shift)

def reference(frames, cotangent, conv_weight, conv_bias, norm_gain, norm_shift, clip_ids):
    channels = frames.shape[-1]
    per_group = channels // GROUPS
    labels = jnp.arange(NCLIP, dtype=jnp.int32)
    member = (clip_ids[:, None] == labels[None, :]).astype(jnp.float32)
    counts = lax.optimization_barrier(jnp.sum(member, axis=0)) * (FR * ROWS * WC * per_group)

    def to_clips(values):
        return lax.optimization_barrier(jnp.sum(member[:, :, None] * values[:, None, :], axis=0)) / counts[:, None]

    def to_spans(values):
        return lax.optimization_barrier(jnp.sum(member[:, :, None] * values[None, :, :], axis=1))

    def group_sum(frame_block):
        return lax.optimization_barrier(jnp.sum(frame_block.astype(jnp.float32).reshape(-1, GROUPS, per_group), axis=(0, 2)))
    group_mean = to_spans(to_clips(lax.map(group_sum, frames)))

    def square_sum(inputs):
        frame_block, center = inputs
        grouped = frame_block.astype(jnp.float32).reshape(-1, GROUPS, per_group) - center[None, :, None]
        return lax.optimization_barrier(jnp.sum(grouped * grouped, axis=(0, 2)))
    inverse_std = to_spans(lax.rsqrt(to_clips(lax.map(square_sum, (frames, group_mean))) + epsilon))

    def activate(inputs):
        frame_block, center, inv_scale = inputs
        normed, lifted = normalize(frame_block, center, inv_scale, norm_gain, norm_shift)
        return jax.nn.silu(lifted).astype(jnp.bfloat16)
    active = lax.map(activate, (frames, group_mean, inverse_std))
    marker = jnp.full((1,), -1, jnp.int32)
    starts = clip_ids != jnp.concatenate([marker, clip_ids[:-1]])
    same_next = clip_ids == jnp.concatenate([clip_ids[1:], marker])
    first_copy = jnp.concatenate([active[:, 0:1], active[:, 0:1]], axis=1)
    last_frames = jnp.concatenate([jnp.zeros_like(first_copy[0:1]), active[:-1, FR - 2:]], axis=0)
    carried = jnp.where(starts[:, None, None, None, None], first_copy, last_frames)
    pad_spec = ((0, 0), (0, 0), (1, 1), (1, 1), (0, 0))
    padded = jnp.pad(jnp.concatenate([carried, active], axis=1), pad_spec)
    kernel = conv_weight.reshape(3, 3, 3 * channels, channels)
    encoded = (lax.map(lambda frame_block: conv_block(frame_block, kernel), padded) + conv_bias).astype(jnp.bfloat16)
    blank_frames = jnp.zeros_like(cotangent[:, 0:2])
    next_frames = jnp.concatenate([cotangent[1:, 0:2], blank_frames[0:1]], axis=0)
    next_frames = jnp.where(same_next[:, None, None, None, None], next_frames, blank_frames)
    cot_padded = jnp.pad(jnp.concatenate([blank_frames, cotangent, next_frames], axis=1), pad_spec)
    flipped = jnp.swapaxes(conv_weight[::-1, ::-1, ::-1], 3, 4).reshape(3, 3, 3 * channels, channels)
    adjoint_ext = lax.map(lambda frame_block: conv_block(frame_block, flipped), cot_padded)
    start_term = jnp.where(starts[:, None, None, None], adjoint_ext[:, 0] + adjoint_ext[:, 1], 0.0)
    adjoint = jnp.concatenate([adjoint_ext[:, 2:3] + start_term[:, None], adjoint_ext[:, 3:]], axis=1)

    def backward_parts(frame_block, adjoint_block, center, inv_scale):
        normed, lifted = normalize(frame_block, center, inv_scale, norm_gain, norm_shift)
        sigmoid_val = jax.nn.sigmoid(lifted)
        pre_grad = adjoint_block * sigmoid_val * (1.0 + lifted * (1.0 - sigmoid_val))
        scaled = (pre_grad * norm_gain).reshape(-1, GROUPS, per_group)
        return (normed, pre_grad, scaled)

    def local_terms(inputs):
        frame_block, adjoint_block, center, inv_scale = inputs
        normed, pre_grad, scaled = backward_parts(frame_block, adjoint_block, center, inv_scale)
        normed_grouped = normed.reshape(-1, GROUPS, per_group)
        return (lax.optimization_barrier(jnp.sum(scaled, axis=(0, 2))), lax.optimization_barrier(jnp.sum(scaled * normed_grouped, axis=(0, 2))), lax.optimization_barrier(jnp.sum((pre_grad * normed).reshape(-1, channels), axis=0)), lax.optimization_barrier(jnp.sum(pre_grad.reshape(-1, channels), axis=0)))
    first_terms, second_terms, gain_terms, shift_terms = lax.map(local_terms, (frames, adjoint, group_mean, inverse_std))
    first_mean = to_spans(to_clips(first_terms))
    second_mean = to_spans(to_clips(second_terms))

    def input_grad(inputs):
        frame_block, adjoint_block, center, inv_scale, mean_one, mean_two = inputs
        normed, pre_grad, scaled = backward_parts(frame_block, adjoint_block, center, inv_scale)
        normed_grouped = normed.reshape(-1, GROUPS, per_group)
        result = inv_scale[None, :, None] * (scaled - mean_one[None, :, None] - normed_grouped * mean_two[None, :, None])
        return result.reshape(frame_block.shape).astype(jnp.bfloat16)
    frames_grad = lax.map(input_grad, (frames, adjoint, group_mean, inverse_std, first_mean, second_mean))

    def accumulate(running, inputs):
        frame_block, cot_block = inputs
        return (running + weight_block(frame_block, cot_block), None)
    weight_sum = lax.scan(accumulate, jnp.zeros(conv_weight.shape, jnp.float32), (padded, cotangent))[0]
    factor = 1.0 / math.sqrt(POSITIONS)
    bias_sum = lax.optimization_barrier(jnp.sum(cotangent.astype(jnp.float32).reshape(-1, channels), axis=0))
    return (encoded, frames_grad, weight_sum * factor, bias_sum * factor, lax.optimization_barrier(jnp.sum(gain_terms, axis=0)) * factor, lax.optimization_barrier(jnp.sum(shift_terms, axis=0)) * factor)
```

```python
import functools
import math

import jax
import jax.numpy as jnp
from jax import lax
from jax.experimental import pallas as pl
from jax.experimental.pallas import tpu as pltpu
from jax.sharding import PartitionSpec as P

MESH = pl.DeviceIdType.MESH
F32 = jnp.float32
BF16 = jnp.bfloat16

NX, NY, NZ, NC = 4, 4, 8, 2
SPANS = NX * NZ * NC
PLANE = NX * NY
LINE = NZ * NC
C = 128
PER_GROUP = 4
FR = 4
RB = 2
W = 128
EPSILON = 1e-06
POSITIONS = SPANS * FR * RB * NY * W
PER_DEVICE = FR * RB * W * PER_GROUP
PER_SPAN = PER_DEVICE * NY
TAP_ROWS = 27 * C
HALF = TAP_ROWS // 2
CHUNK = 112
REGION = PLANE * CHUNK

(S_P1, S_P2, S_FH, S_CH, S_CORE, S_XY, S_Z, S_GXY, S_GCORE, S_Q1, S_Q2) = range(11)


def group_sum(v):
    lane = lax.broadcasted_iota(jnp.int32, v.shape, 1)
    pair = v + jnp.where(lane % 2 == 0, pltpu.roll(v, 127, axis=1), pltpu.roll(v, 1, axis=1))
    return pair + jnp.where(lane % 4 < 2, pltpu.roll(pair, 126, axis=1), pltpu.roll(pair, 2, axis=1))


def distance(d, n):
    return min(d, n - d)


PLANE_OFFS = sorted(
    [(a, b) for a in range(NX) for b in range(NY) if (a, b) != (0, 0)],
    key=lambda o: -(distance(o[0], NX) + distance(o[1], NY)),
)
LINE_OFFS = sorted(
    [(a, b) for a in range(NZ) for b in range(NC) if (a, b) != (0, 0)],
    key=lambda o: -(4 * distance(o[0], NZ) + o[1]),
)
Z_OFFS = sorted(range(1, NZ), key=lambda o: -distance(o, NZ))


def wait_for(ref, sem):
    pltpu.make_async_copy(ref, ref, sem).wait()


def shifted(v, back):
    row = lax.broadcasted_iota(jnp.int32, v.shape, 0)
    if back:
        return jnp.where(row == 0, 0.0, pltpu.roll(v, 1, axis=0))
    return jnp.where(row == W - 1, 0.0, pltpu.roll(v, W - 1, axis=0))


def rows_sum(v):
    return jnp.sum(v.reshape(W // 8, 8, C), axis=0)


def kernel(
    frames, cot, wt, bias, gain, shift, clip,
    enc_out, fg_out, wg_out, small_out,
    fp_buf, cp_buf, act, act_t, act_st, cot_st, wcat,
    p1_src, p1, p2_src, p2, q1_src, q1, q2_src, q2, masks,
    grads, r_core, s_xy, r_xy, r_z, t_xy, t_core, acc,
    send, recv,
):
    span = lax.axis_index("span")
    y = lax.axis_index("space")
    x = lax.div(span, LINE)
    line = lax.rem(span, LINE)
    z = lax.div(line, NC)
    c = lax.rem(span, NC)
    plane = x * NY + y

    def in_plane(o):
        return (lax.rem(x + o[0], NX) * LINE + line, lax.rem(y + o[1], NY))

    def in_line(o):
        return (x * LINE + lax.rem(z + o[0], NZ) * NC + lax.rem(c + o[1], NC), y)

    def beside(ds, dy):
        return (lax.rem(span + ds + SPANS, SPANS), lax.rem(y + dy + NY, NY))

    def push(src, dst, which, device):
        pltpu.make_async_remote_copy(
            src_ref=src, dst_ref=dst, send_sem=send.at[which], recv_sem=recv.at[which],
            device_id=device, device_id_type=MESH,
        ).start()

    barrier = pltpu.get_barrier_semaphore()
    partners = [in_plane(o) for o in PLANE_OFFS] + [in_line(o) for o in LINE_OFFS]
    partners += [beside(ds, dy) for ds in (-1, 1) for dy in (-1, 0, 1)]
    for device in partners:
        pl.semaphore_signal(barrier, inc=1, device_id=device, device_id_type=MESH)

    def add_rows(j, total):
        return total + rows_sum(frames[0, j // RB, j % RB].astype(F32))

    total = lax.fori_loop(0, FR * RB, add_rows, jnp.zeros((8, C), F32))
    mean_here = group_sum(jnp.sum(total, axis=0, keepdims=True)) * (1.0 / PER_DEVICE)

    def add_squares(j, total):
        v = frames[0, j // RB, j % RB].astype(F32) - mean_here
        return total + rows_sum(v * v)

    total = lax.fori_loop(0, FR * RB, add_squares, jnp.zeros((8, C), F32))
    squares_here = group_sum(jnp.sum(total, axis=0, keepdims=True))
    block = jnp.concatenate([mean_here, squares_here, jnp.zeros((6, C), F32)], axis=0)
    p1_src[...] = block
    p1[plane] = block

    pl.semaphore_wait(barrier, len(partners))
    for o in PLANE_OFFS:
        push(p1_src, p1.at[plane], S_P1, in_plane(o))
    push(frames.at[0, :, 1], fp_buf.at[pl.ds(2, FR), 0], S_FH, beside(0, 1))
    push(frames.at[0, :, 0], fp_buf.at[pl.ds(2, FR), 3], S_FH, beside(0, -1))
    push(frames.at[0, pl.ds(2, 2)], fp_buf.at[pl.ds(0, 2), pl.ds(1, RB)], S_FH, beside(1, 0))
    push(frames.at[0, pl.ds(2, 2), 1], fp_buf.at[pl.ds(0, 2), 0], S_FH, beside(1, 1))
    push(frames.at[0, pl.ds(2, 2), 0], fp_buf.at[pl.ds(0, 2), 3], S_FH, beside(1, -1))

    own = clip[span]
    before = clip[lax.rem(span + SPANS - 1, SPANS)]
    after = clip[lax.rem(span + 1, SPANS)]
    starts = jnp.where((span == 0) | (before != own), 1.0, 0.0).astype(F32)
    same_next = jnp.where((span < SPANS - 1) & (after == own), 1.0, 0.0).astype(F32)
    above = jnp.where(y > 0, 1.0, 0.0).astype(F32)
    below = jnp.where(y < NY - 1, 1.0, 0.0).astype(F32)

    sub = lax.broadcasted_iota(jnp.int32, (8, C), 0)

    def fill_masks(k, count):
        block = jnp.zeros((8, C), F32)
        for a in range(NX):
            member = jnp.where(clip[a * LINE + k] == own, 1.0, 0.0).astype(F32)
            block = block + jnp.where(sub % 4 == a, member, 0.0)
            count = count + member
        masks[k] = block
        return count

    spans_here = lax.fori_loop(0, LINE, fill_masks, jnp.float32(0.0))
    spans_row = jnp.zeros((1, C), F32) + spans_here
    inv_count = 1.0 / (spans_row * PER_SPAN)

    def stack_cot(v, f, r):
        cot_st[f, r, :, 0:C] = shifted(v, False).astype(BF16)
        cot_st[f, r, :, C:2 * C] = v.astype(BF16)
        cot_st[f, r, :, 2 * C:3 * C] = shifted(v, True).astype(BF16)

    def stack_own(f, total):
        for r in range(RB):
            v = cot[0, f, r].astype(F32)
            total = total + rows_sum(v)
            stack_cot(v, f, r + 1)
            fp_buf[f + 2, r + 1] = frames[0, f, r]
        return total

    bias_terms = lax.fori_loop(0, FR, stack_own, jnp.zeros((8, C), F32))
    bias_terms = jnp.sum(bias_terms, axis=0, keepdims=True)

    wait_for(p1.at[pl.ds(0, PLANE - 1)], recv.at[S_P1])
    mean_rows, square_rows = [], []
    for a in range(NX):
        parts = [p1[a * NY + b] for b in range(NY)]
        summed = parts[0] + parts[1] + parts[2] + parts[3]
        mean = summed[0:1] * (1.0 / NY)
        spread = sum((q[0:1] - mean) * (q[0:1] - mean) for q in parts)
        mean_rows.append(mean)
        square_rows.append(summed[1:2] + PER_DEVICE * spread)
    block = jnp.concatenate(mean_rows + square_rows, axis=0)
    p2_src[...] = block
    p2[line] = block
    for o in LINE_OFFS:
        push(p2_src, p2.at[line], S_P2, in_line(o))
    push(cot.at[0, :, 1], cp_buf.at[pl.ds(0, FR), 0], S_CH, beside(0, 1))
    push(cot.at[0, :, 0], cp_buf.at[pl.ds(0, FR), 3], S_CH, beside(0, -1))
    push(cot.at[0, pl.ds(0, 2)], cp_buf.at[pl.ds(4, 2), pl.ds(1, RB)], S_CH, beside(-1, 0))
    push(cot.at[0, pl.ds(0, 2), 1], cp_buf.at[pl.ds(4, 2), 0], S_CH, beside(-1, 1))
    push(cot.at[0, pl.ds(0, 2), 0], cp_buf.at[pl.ds(4, 2), 3], S_CH, beside(-1, -1))

    def widen(t, carry):
        for ds in range(3):
            wcat[t, :, ds * C:(ds + 1) * C] = wt[t, pl.ds(ds * C, C)]
        return carry

    lax.fori_loop(0, 9, widen, 0)

    wait_for(fp_buf.at[pl.ds(0, 4)], recv.at[S_FH])

    def carry_rows(r, carry):
        first = fp_buf[2, r].astype(F32) * starts
        for f in range(2):
            fp_buf[f, r] = (first + fp_buf[f, r].astype(F32) * (1.0 - starts)).astype(BF16)
        return carry

    lax.fori_loop(0, RB + 2, carry_rows, 0)

    wait_for(p2.at[pl.ds(0, LINE - 1)], recv.at[S_P2])
    summed = jnp.zeros((8, C), F32)
    for k in range(LINE):
        summed = summed + p2[k] * masks[k]
    mean = jnp.sum(summed[0:4], axis=0, keepdims=True) / spans_row
    squares = jnp.sum(summed[4:8], axis=0, keepdims=True)
    spread = jnp.zeros((8, C), F32)
    for k in range(LINE):
        off = p2[k] - mean
        spread = spread + off * off * masks[k]
    squares = squares + PER_SPAN * jnp.sum(spread[0:4], axis=0, keepdims=True)
    inverse_std = lax.rsqrt(squares * inv_count + EPSILON)
    gain_row = gain[...]
    shift_row = shift[...]
    lift = inverse_std * gain_row

    def activate(f, carry):
        for r in range(RB + 2):
            lifted = (fp_buf[f, r].astype(F32) - mean) * lift + shift_row
            a = lifted / (1.0 + jnp.exp(-lifted))
            if r == 0:
                a = a * above
            if r == RB + 1:
                a = a * below
            act[f, r] = a.astype(BF16)
            flat = a.T.astype(BF16)
            for k in range(RB):
                dr = r - k
                if 0 <= dr < 3:
                    act_t[f, dr * C:(dr + 1) * C, k * W:(k + 1) * W] = flat
        return carry

    lax.fori_loop(0, FR + 2, activate, 0)

    def tap_grad(t, carry):
        left = jnp.concatenate([act_t[t + f] for f in range(FR)], axis=1)
        right = cot_st[0:FR, 1:1 + RB].reshape(FR * RB * W, 3 * C)
        g = jnp.dot(left, right, preferred_element_type=F32)
        for dr in range(3):
            for ds in range(3):
                piece = g[dr * C:(dr + 1) * C, ds * C:(ds + 1) * C].astype(BF16)
                grads[pl.ds(pl.multiple_of(t * 9 * C + (dr * 3 + ds) * C, C), C)] = piece
        return carry

    lax.fori_loop(0, 3, tap_grad, 0)
    other = pl.multiple_of((1 - c) * HALF, 64)
    push(grads.at[pl.ds(other, HALF)], r_core, S_CORE, in_line((0, 1)))
    s_xy[HALF:REGION] = jnp.zeros((REGION - HALF, C), BF16)
    wait_for(r_core, recv.at[S_CORE])
    mine = pl.multiple_of(c * HALF, 64)

    def add_core(k, carry):
        at = pl.multiple_of(k * 64, 64)
        own_part = grads[pl.ds(pl.multiple_of(mine + at, 64), 64)].astype(F32)
        s_xy[pl.ds(at, 64)] = (own_part + r_core[pl.ds(at, 64)].astype(F32)).astype(BF16)
        return carry

    lax.fori_loop(0, HALF // 64, add_core, 0)
    for o in PLANE_OFFS:
        px, py = lax.rem(x + o[0], NX), lax.rem(y + o[1], NY)
        at = pl.multiple_of((px * NY + py) * CHUNK, 16)
        push(s_xy.at[pl.ds(at, CHUNK)], r_xy.at[plane], S_XY, in_plane(o))
    r_xy[plane] = s_xy[pl.ds(pl.multiple_of(plane * CHUNK, 16), CHUNK)]

    wait_for(cp_buf.at[pl.ds(0, 4)], recv.at[S_CH])

    def stack_sides(f, carry):
        stack_cot(cp_buf[f, 0].astype(F32) * above, f, 0)
        stack_cot(cp_buf[f, 3].astype(F32) * below, f, 3)
        return carry

    lax.fori_loop(0, FR, stack_sides, 0)

    def stack_next(f, carry):
        for r in range(RB + 2):
            edge = above if r == 0 else below if r == RB + 1 else 1.0
            stack_cot(cp_buf[f, r].astype(F32) * (same_next * edge), f, r)
        return carry

    lax.fori_loop(FR, FR + 2, stack_next, 0)

    acc[...] = jnp.zeros_like(acc)

    def contract(window, k):
        return lax.dot_general(
            window, k, (((1,), (1,)), ((), ())), preferred_element_type=F32
        )

    def adjoint_tap(t, carry):
        dt, dr = lax.div(t, 3), lax.rem(t, 3)
        window = cot_st[pl.ds(2 - dt, FR), pl.ds(2 - dr, RB)].reshape(FR * RB * W, 3 * C)
        acc[...] += contract(window, wcat[t])
        return carry

    lax.fori_loop(0, 9, adjoint_tap, 0)

    def front_tap(dr, carry):
        zero = cot_st[0, pl.ds(2 - dr, RB)].reshape(RB * W, 3 * C)
        one = cot_st[1, pl.ds(2 - dr, RB)].reshape(RB * W, 3 * C)
        front = contract(zero, wcat[dr]) + contract(one, wcat[dr]) + contract(zero, wcat[dr + 3])
        acc[0:RB * W] += starts * front
        return carry

    lax.fori_loop(0, 3, front_tap, 0)

    def pre_grads(j, sums):
        at = pl.ds(pl.multiple_of(j * W, W), W)
        normed = (frames[0, j // RB, j % RB].astype(F32) - mean) * inverse_std
        lifted = normed * gain_row + shift_row
        s = 1.0 / (1.0 + jnp.exp(-lifted))
        pre = acc[at] * s * (1.0 + lifted * (1.0 - s))
        acc[at] = pre
        return sums[0] + rows_sum(pre), sums[1] + rows_sum(pre * normed)

    zero = jnp.zeros((8, C), F32)
    shift_terms, gain_terms = lax.fori_loop(0, FR * RB, pre_grads, (zero, zero))
    shift_terms = jnp.sum(shift_terms, axis=0, keepdims=True)
    gain_terms = jnp.sum(gain_terms, axis=0, keepdims=True)
    block = jnp.concatenate([shift_terms, gain_terms, bias_terms, jnp.zeros((5, C), F32)], axis=0)
    q1_src[...] = block
    q1[plane] = block
    for o in PLANE_OFFS:
        push(q1_src, q1.at[plane], S_Q1, in_plane(o))

    wait_for(r_xy.at[pl.ds(0, PLANE - 1)], recv.at[S_XY])
    total = r_xy[0].astype(F32)
    for k in range(1, PLANE):
        total = total + r_xy[k].astype(F32)
    r_z[z] = total.astype(BF16)
    for o in Z_OFFS:
        push(r_z.at[z], r_z.at[z], S_Z, in_line((o, 0)))

    def stack_act(f, carry):
        for r in range(RB + 2):
            v = act[f, r].astype(F32)
            act_st[f, r, :, 0:C] = shifted(v, True).astype(BF16)
            act_st[f, r, :, C:2 * C] = act[f, r]
            act_st[f, r, :, 2 * C:3 * C] = shifted(v, False).astype(BF16)
        return carry

    lax.fori_loop(0, FR + 2, stack_act, 0)

    wait_for(q1.at[pl.ds(0, PLANE - 1)], recv.at[S_Q1])
    rows = []
    bias_sum = jnp.zeros((1, C), F32)
    for a in range(NX):
        summed = q1[a * NY] + q1[a * NY + 1] + q1[a * NY + 2] + q1[a * NY + 3]
        rows.append(summed)
        bias_sum = bias_sum + summed[2:3]
    block = jnp.concatenate(
        [q[0:1] for q in rows] + [q[1:2] for q in rows] + [bias_sum, jnp.zeros((7, C), F32)], axis=0
    )
    q2_src[...] = block
    q2[line] = block
    for o in LINE_OFFS:
        push(q2_src, q2.at[line], S_Q2, in_line(o))

    wait_for(r_z.at[pl.ds(0, NZ - 1)], recv.at[S_Z])
    total = r_z[0].astype(F32)
    for k in range(1, NZ):
        total = total + r_z[k].astype(F32)
    t_xy[plane] = total.astype(BF16)
    for o in PLANE_OFFS:
        push(t_xy.at[plane], t_xy.at[plane], S_GXY, in_plane(o))


    wait_for(q2.at[pl.ds(0, LINE - 1)], recv.at[S_Q2])
    summed = jnp.zeros((8, C), F32)
    whole = jnp.zeros((16, C), F32)
    for k in range(LINE):
        part = q2[k]
        whole = whole + part
        summed = summed + part[0:8] * masks[k]
    first_mean = group_sum(jnp.sum(summed[0:4], axis=0, keepdims=True) * gain_row) * inv_count
    second_mean = group_sum(jnp.sum(summed[4:8], axis=0, keepdims=True) * gain_row) * inv_count
    factor = 1.0 / math.sqrt(POSITIONS)
    small_out[...] = jnp.concatenate(
        [
            whole[8:9],
            jnp.sum(whole[4:8], axis=0, keepdims=True),
            jnp.sum(whole[0:4], axis=0, keepdims=True),
            jnp.zeros((5, C), F32),
        ],
        axis=0,
    ) * factor

    def frame_grads(j, carry):
        at = pl.ds(pl.multiple_of(j * W, W), W)
        normed = (frames[0, j // RB, j % RB].astype(F32) - mean) * inverse_std
        result = inverse_std * (acc[at] * gain_row - first_mean - normed * second_mean)
        fg_out[0, j // RB, j % RB] = result.astype(BF16)
        return carry

    lax.fori_loop(0, FR * RB, frame_grads, 0)

    acc[...] = jnp.zeros_like(acc) + bias[...]

    def forward_tap(t, carry):
        dt, dr = lax.div(t, 3), lax.rem(t, 3)
        window = act_st[pl.ds(dt, FR), pl.ds(dr, RB)].reshape(FR * RB * W, 3 * C)
        acc[...] += jnp.dot(window, wt[t], preferred_element_type=F32)
        return carry

    lax.fori_loop(0, 9, forward_tap, 0)
    enc_out[0] = acc[...].astype(BF16).reshape(FR, RB, W, C)

    wait_for(t_xy.at[pl.ds(0, PLANE - 1)], recv.at[S_GXY])
    push(t_xy, t_core, S_GCORE, in_line((0, 1)))

    def write(src, base):
        at = pl.multiple_of(base, 64)
        wg_out[pl.ds(at, HALF)] = src[...].reshape(REGION, C)[0:HALF]

    write(t_xy, c * HALF)
    wait_for(t_core, recv.at[S_GCORE])
    write(t_core, (1 - c) * HALF)

    wait_for(p1.at[pl.ds(0, PLANE - 1)], send.at[S_P1])
    wait_for(p2.at[pl.ds(0, LINE - 1)], send.at[S_P2])
    wait_for(fp_buf.at[pl.ds(0, 4)], send.at[S_FH])
    wait_for(cp_buf.at[pl.ds(0, 4)], send.at[S_CH])
    wait_for(r_core, send.at[S_CORE])
    wait_for(r_xy.at[pl.ds(0, PLANE - 1)], send.at[S_XY])
    wait_for(r_z.at[pl.ds(0, NZ - 1)], send.at[S_Z])
    wait_for(t_xy.at[pl.ds(0, PLANE - 1)], send.at[S_GXY])
    wait_for(t_core, send.at[S_GCORE])
    wait_for(q1.at[pl.ds(0, PLANE - 1)], send.at[S_Q1])
    wait_for(q2.at[pl.ds(0, LINE - 1)], send.at[S_Q2])


def local(frames, cotangent, conv_weight, conv_bias, norm_gain, norm_shift, clip_ids):
    vmem = pl.BlockSpec(memory_space=pltpu.VMEM)
    smem = pl.BlockSpec(memory_space=pltpu.SMEM)
    enc, fg, wg, small = pl.pallas_call(
        kernel,
        out_shape=(
            jax.ShapeDtypeStruct(frames.shape, BF16),
            jax.ShapeDtypeStruct(frames.shape, BF16),
            jax.ShapeDtypeStruct((TAP_ROWS, C), BF16),
            jax.ShapeDtypeStruct((8, C), F32),
        ),
        in_specs=[vmem] * 6 + [smem],
        out_specs=(vmem,) * 4,
        scratch_shapes=[
            pltpu.VMEM((FR + 2, RB + 2, W, C), BF16),
            pltpu.VMEM((FR + 2, RB + 2, W, C), BF16),
            pltpu.VMEM((FR + 2, RB + 2, W, C), BF16),
            pltpu.VMEM((FR + 2, 3 * C, RB * W), BF16),
            pltpu.VMEM((FR + 2, RB + 2, W, 3 * C), BF16),
            pltpu.VMEM((FR + 2, RB + 2, W, 3 * C), BF16),
            pltpu.VMEM((9, C, 3 * C), BF16),
            pltpu.VMEM((8, C), F32),
            pltpu.VMEM((PLANE, 8, C), F32),
            pltpu.VMEM((8, C), F32),
            pltpu.VMEM((LINE, 8, C), F32),
            pltpu.VMEM((8, C), F32),
            pltpu.VMEM((PLANE, 8, C), F32),
            pltpu.VMEM((16, C), F32),
            pltpu.VMEM((LINE, 16, C), F32),
            pltpu.VMEM((LINE, 8, C), F32),
            pltpu.VMEM((TAP_ROWS, C), BF16),
            pltpu.VMEM((HALF, C), BF16),
            pltpu.VMEM((REGION, C), BF16),
            pltpu.VMEM((PLANE, CHUNK, C), BF16),
            pltpu.VMEM((NZ, CHUNK, C), BF16),
            pltpu.VMEM((PLANE, CHUNK, C), BF16),
            pltpu.VMEM((PLANE, CHUNK, C), BF16),
            pltpu.VMEM((FR * RB * W, C), F32),
            pltpu.SemaphoreType.DMA((11,)),
            pltpu.SemaphoreType.DMA((11,)),
        ],
        compiler_params=pltpu.CompilerParams(
            collective_id=0, has_side_effects=True, vmem_limit_bytes=48 * 2**20
        ),
        cost_estimate=pl.CostEstimate(flops=3 * 10**9, bytes_accessed=4 * 10**6, transcendentals=10**6),
        name="block",
    )(
        frames,
        cotangent,
        conv_weight.reshape(9, 3 * C, C),
        conv_bias.reshape(1, C),
        norm_gain.reshape(1, C),
        norm_shift.reshape(1, C),
        clip_ids,
    )
    factor = 1.0 / math.sqrt(POSITIONS)
    weight_grad = wg.astype(F32).reshape(3, 3, 3, C, C) * factor
    return enc, fg, weight_grad, small[0], small[1], small[2]


def solution(mesh):
    placed = (P("span", None, "space", None, None),) * 2 + (P(),) * 5
    return jax.shard_map(
        local,
        mesh=mesh,
        in_specs=placed,
        out_specs=(P("span", None, "space", None, None),) * 2 + (P(),) * 4,
        check_vma=False,
    )
```

```python
import math

import jax
import jax.numpy as jnp
from jax import lax
from jax.experimental import pallas as pl
from jax.experimental.pallas import tpu as pltpu
from jax.sharding import PartitionSpec as P

MESH = pl.DeviceIdType.MESH
F32 = jnp.float32
BF16 = jnp.bfloat16

NX, NY, NZ, NC = 4, 4, 8, 2
SPANS = NX * NZ * NC
PLANE = NX * NY
LINE = NZ * NC
C = 128
PER_GROUP = 4
FR = 4
RB = 2
W = 128
EPSILON = 1e-06
POSITIONS = SPANS * FR * RB * NY * W
PER_DEVICE = FR * RB * W * PER_GROUP
PER_SPAN = PER_DEVICE * NY
TAP_ROWS = 27 * C
HALF = TAP_ROWS // 2
CHUNK = 112
REGION = PLANE * CHUNK

PARTS = (64, 48)
STARTS = (0, PLANE * PARTS[0])

(S_P1, S_P2, S_FH, S_CH, S_CORE, S_Q1, S_Q2) = range(7)
S_XY, S_Z, S_GXY, S_GCORE = (7, 8), (9, 10), (11, 12), (13, 14)
SEMS = 15


def group_sum(v):
    lane = lax.broadcasted_iota(jnp.int32, v.shape, 1)
    pair = v + jnp.where(lane % 2 == 0, pltpu.roll(v, 127, axis=1), pltpu.roll(v, 1, axis=1))
    return pair + jnp.where(lane % 4 < 2, pltpu.roll(pair, 126, axis=1), pltpu.roll(pair, 2, axis=1))


def distance(d, n):
    return min(d, n - d)


PLANE_OFFS = sorted(
    [(a, b) for a in range(NX) for b in range(NY) if (a, b) != (0, 0)],
    key=lambda o: -(distance(o[0], NX) + distance(o[1], NY)),
)
LINE_OFFS = sorted(
    [(a, b) for a in range(NZ) for b in range(NC) if (a, b) != (0, 0)],
    key=lambda o: -(4 * distance(o[0], NZ) + o[1]),
)
Z_OFFS = sorted(range(1, NZ), key=lambda o: -distance(o, NZ))


def wait_for(ref, sem):
    pltpu.make_async_copy(ref, ref, sem).wait()


def shifted(v, back):
    row = lax.broadcasted_iota(jnp.int32, v.shape, 0)
    if back:
        return jnp.where(row == 0, 0.0, pltpu.roll(v, 1, axis=0))
    return jnp.where(row == W - 1, 0.0, pltpu.roll(v, W - 1, axis=0))


def rows_sum(v):
    return jnp.sum(v.reshape(W // 8, 8, C), axis=0)


def kernel(
    frames_hbm, cot_hbm, wt_hbm, bias_hbm, gain_hbm, shift_hbm, clip_hbm,
    enc_out, fg_out, wg_out, small_out,
    frames, cot, wt, bias, gain, shift, clip, fp_buf, cp_buf, act, act_t, act_st, cot_st, wcat,
    p1_src, p1, p2_src, p2, q1_src, q1, q2_src, q2, masks,
    grads, r_core, s_xy, r_xy0, r_xy1, r_z0, r_z1, t_xy0, t_xy1, t_core0, t_core1, acc, out_acc,
    send, recv, load,
):
    arrays = (
        (frames_hbm, frames), (clip_hbm, clip), (cot_hbm, cot), (gain_hbm, gain),
        (shift_hbm, shift), (bias_hbm, bias), (wt_hbm, wt),
    )
    loads = [pltpu.make_async_copy(a, b, load.at[i]) for i, (a, b) in enumerate(arrays)]
    loads[0].start()
    r_xy, r_z, t_xy, t_core = (r_xy0, r_xy1), (r_z0, r_z1), (t_xy0, t_xy1), (t_core0, t_core1)
    sent, arrived = [], set()

    def receive(ref, which):
        wait_for(ref, recv.at[which])
        arrived.add(which)

    def finish():
        for ref, which in sent:
            wait_for(ref, send.at[which])
            if which not in arrived:
                receive(ref, which)

    span = lax.axis_index("span")
    y = lax.axis_index("space")
    x = lax.div(span, LINE)
    line = lax.rem(span, LINE)
    z = lax.div(line, NC)
    c = lax.rem(span, NC)
    plane = x * NY + y

    def in_plane(o):
        return (lax.rem(x + o[0], NX) * LINE + line, lax.rem(y + o[1], NY))

    def in_line(o):
        return (x * LINE + lax.rem(z + o[0], NZ) * NC + lax.rem(c + o[1], NC), y)

    def beside(ds, dy):
        return (lax.rem(span + ds + SPANS, SPANS), lax.rem(y + dy + NY, NY))

    def push(src, dst, which, device):
        pltpu.make_async_remote_copy(
            src_ref=src, dst_ref=dst, send_sem=send.at[which], recv_sem=recv.at[which],
            device_id=device, device_id_type=MESH,
        ).start()

    barrier = pltpu.get_barrier_semaphore()
    partners = [in_plane(o) for o in PLANE_OFFS] + [in_line(o) for o in LINE_OFFS]
    partners += [beside(ds, dy) for ds in (-1, 1) for dy in (-1, 0, 1)]
    for device in partners:
        pl.semaphore_signal(barrier, inc=1, device_id=device, device_id_type=MESH)

    for copy in loads[1:]:
        copy.start()

    loads[0].wait()

    def add_rows(j, total):
        return total + rows_sum(frames[0, j // RB, j % RB].astype(F32))

    total = lax.fori_loop(0, FR * RB, add_rows, jnp.zeros((8, C), F32))
    mean_here = group_sum(jnp.sum(total, axis=0, keepdims=True)) * (1.0 / PER_DEVICE)

    def add_squares(j, total):
        v = frames[0, j // RB, j % RB].astype(F32) - mean_here
        return total + rows_sum(v * v)

    total = lax.fori_loop(0, FR * RB, add_squares, jnp.zeros((8, C), F32))
    squares_here = group_sum(jnp.sum(total, axis=0, keepdims=True))
    block = jnp.concatenate([mean_here, squares_here, jnp.zeros((6, C), F32)], axis=0)
    p1_src[...] = block
    p1[plane] = block

    pl.semaphore_wait(barrier, len(partners))
    for o in PLANE_OFFS:
        push(p1_src, p1.at[plane], S_P1, in_plane(o))
    sent.append((p1.at[pl.ds(0, PLANE - 1)], S_P1))
    push(frames.at[0, :, 1], fp_buf.at[pl.ds(2, FR), 0], S_FH, beside(0, 1))
    push(frames.at[0, :, 0], fp_buf.at[pl.ds(2, FR), 3], S_FH, beside(0, -1))
    push(frames.at[0, pl.ds(2, 2)], fp_buf.at[pl.ds(0, 2), pl.ds(1, RB)], S_FH, beside(1, 0))
    push(frames.at[0, pl.ds(2, 2), 1], fp_buf.at[pl.ds(0, 2), 0], S_FH, beside(1, 1))
    push(frames.at[0, pl.ds(2, 2), 0], fp_buf.at[pl.ds(0, 2), 3], S_FH, beside(1, -1))

    sent.append((fp_buf.at[pl.ds(0, 4)], S_FH))
    for copy in loads[1:]:
        copy.wait()

    for r in range(NC):
        grads[r * REGION + HALF:(r + 1) * REGION] = jnp.zeros((REGION - HALF, C), F32)
    r_core[HALF:REGION] = jnp.zeros((REGION - HALF, C), F32)

    own = clip[span]
    before = clip[lax.rem(span + SPANS - 1, SPANS)]
    after = clip[lax.rem(span + 1, SPANS)]
    starts = jnp.where((span == 0) | (before != own), 1.0, 0.0).astype(F32)
    same_next = jnp.where((span < SPANS - 1) & (after == own), 1.0, 0.0).astype(F32)
    above = jnp.where(y > 0, 1.0, 0.0).astype(F32)
    below = jnp.where(y < NY - 1, 1.0, 0.0).astype(F32)

    sub = lax.broadcasted_iota(jnp.int32, (8, C), 0)

    def fill_masks(k, count):
        block = jnp.zeros((8, C), F32)
        for a in range(NX):
            member = jnp.where(clip[a * LINE + k] == own, 1.0, 0.0).astype(F32)
            block = block + jnp.where(sub % 4 == a, member, 0.0)
            count = count + member
        masks[k] = block
        return count

    spans_here = lax.fori_loop(0, LINE, fill_masks, jnp.float32(0.0))
    spans_row = jnp.zeros((1, C), F32) + spans_here
    inv_count = 1.0 / (spans_row * PER_SPAN)

    def stack_cot(v, f, r):
        cot_st[f, r, :, 0:C] = shifted(v, False).astype(BF16)
        cot_st[f, r, :, C:2 * C] = v.astype(BF16)
        cot_st[f, r, :, 2 * C:3 * C] = shifted(v, True).astype(BF16)

    def stack_own(f, total):
        for r in range(RB):
            v = cot[0, f, r].astype(F32)
            total = total + rows_sum(v)
            stack_cot(v, f, r + 1)
            fp_buf[f + 2, r + 1] = frames[0, f, r]
        return total

    bias_terms = lax.fori_loop(0, FR, stack_own, jnp.zeros((8, C), F32))
    bias_terms = jnp.sum(bias_terms, axis=0, keepdims=True)

    receive(p1.at[pl.ds(0, PLANE - 1)], S_P1)
    mean_rows, square_rows = [], []
    for a in range(NX):
        parts = [p1[a * NY + b] for b in range(NY)]
        summed = parts[0] + parts[1] + parts[2] + parts[3]
        mean = summed[0:1] * (1.0 / NY)
        spread = sum((q[0:1] - mean) * (q[0:1] - mean) for q in parts)
        mean_rows.append(mean)
        square_rows.append(summed[1:2] + PER_DEVICE * spread)
    block = jnp.concatenate(mean_rows + square_rows, axis=0)
    p2_src[...] = block
    p2[line] = block
    for o in LINE_OFFS:
        push(p2_src, p2.at[line], S_P2, in_line(o))
    sent.append((p2.at[pl.ds(0, LINE - 1)], S_P2))
    push(cot.at[0, :, 1], cp_buf.at[pl.ds(0, FR), 0], S_CH, beside(0, 1))
    push(cot.at[0, :, 0], cp_buf.at[pl.ds(0, FR), 3], S_CH, beside(0, -1))
    push(cot.at[0, pl.ds(0, 2)], cp_buf.at[pl.ds(4, 2), pl.ds(1, RB)], S_CH, beside(-1, 0))
    push(cot.at[0, pl.ds(0, 2), 1], cp_buf.at[pl.ds(4, 2), 0], S_CH, beside(-1, 1))
    push(cot.at[0, pl.ds(0, 2), 0], cp_buf.at[pl.ds(4, 2), 3], S_CH, beside(-1, -1))

    sent.append((cp_buf.at[pl.ds(0, 4)], S_CH))

    def widen(t, carry):
        for ds in range(3):
            wcat[t, :, ds * C:(ds + 1) * C] = wt[t, pl.ds(ds * C, C)]
        return carry

    lax.fori_loop(0, 9, widen, 0)

    receive(fp_buf.at[pl.ds(0, 4)], S_FH)

    def carry_rows(r, carry):
        first = fp_buf[2, r].astype(F32) * starts
        for f in range(2):
            fp_buf[f, r] = (first + fp_buf[f, r].astype(F32) * (1.0 - starts)).astype(BF16)
        return carry

    lax.fori_loop(0, RB + 2, carry_rows, 0)

    receive(p2.at[pl.ds(0, LINE - 1)], S_P2)
    summed = jnp.zeros((8, C), F32)
    for k in range(LINE):
        summed = summed + p2[k] * masks[k]
    mean = jnp.sum(summed[0:4], axis=0, keepdims=True) / spans_row
    squares = jnp.sum(summed[4:8], axis=0, keepdims=True)
    spread = jnp.zeros((8, C), F32)
    for k in range(LINE):
        off = p2[k] - mean
        spread = spread + off * off * masks[k]
    squares = squares + PER_SPAN * jnp.sum(spread[0:4], axis=0, keepdims=True)
    inverse_std = lax.rsqrt(squares * inv_count + EPSILON)
    gain_row = gain[...]
    shift_row = shift[...]
    lift = inverse_std * gain_row

    def activate(f, carry):
        for r in range(RB + 2):
            lifted = (fp_buf[f, r].astype(F32) - mean) * lift + shift_row
            a = lifted / (1.0 + jnp.exp(-lifted))
            if r == 0:
                a = a * above
            if r == RB + 1:
                a = a * below
            act[f, r] = a.astype(BF16)
            flat = a.T.astype(BF16)
            for k in range(RB):
                dr = r - k
                if 0 <= dr < 3:
                    act_t[f, dr * C:(dr + 1) * C, k * W:(k + 1) * W] = flat
        return carry

    lax.fori_loop(0, FR + 2, activate, 0)

    cotangents = cot_st[0:FR, 1:1 + RB].reshape(FR * RB * W, 3 * C)
    for k in range(3):
        t = c * k + (1 - c) * (2 - k)
        left = jnp.concatenate([act_t[t + f] for f in range(FR)], axis=1)
        g = jnp.dot(left, cotangents, preferred_element_type=F32)
        for b in range(9):
            dr, ds = b // 3, b % 3
            piece = g[dr * C:(dr + 1) * C, ds * C:(ds + 1) * C]
            if k != 1:
                at = pl.multiple_of(t * (9 * C + 32) + b * C, 64)
                grads[pl.ds(at, C)] = piece
            elif b != 4:
                at = (9 + b) * C + (REGION - HALF if b > 4 else 0)
                grads[at:at + C] = piece
            else:
                grads[HALF - 64:HALF] = piece[0:64]
                grads[REGION:REGION + 64] = piece[64:128]
        if k < 2:
            size = (9 * C, HALF - 9 * C)[k]
            source = ((1 - c) * 2 * (9 * C + 32), c * 9 * C + (1 - c) * REGION)[k]
            target = ((1 - c) * (HALF - 9 * C), c * 9 * C)[k]
            push(
                grads.at[pl.ds(pl.multiple_of(source, 64), size)],
                r_core.at[pl.ds(pl.multiple_of(target, 64), size)],
                S_CORE, in_line((0, 1)),
            )
    sent.append((r_core.at[pl.ds(0, HALF)], S_CORE))
    receive(r_core.at[pl.ds(0, HALF)], S_CORE)
    mine = c * REGION

    def both_cores(at, rows):
        a = grads[pl.ds(pl.multiple_of(mine + at, 16), rows)]
        return (a + r_core[pl.ds(pl.multiple_of(at, 16), rows)]).astype(BF16)

    for h, rows in enumerate(PARTS):
        for o in PLANE_OFFS:
            px, py = lax.rem(x + o[0], NX), lax.rem(y + o[1], NY)
            at = pl.multiple_of(STARTS[h] + (px * NY + py) * rows, 16)
            s_xy[pl.ds(at, rows)] = both_cores(at, rows)
            push(s_xy.at[pl.ds(at, rows)], r_xy[h].at[plane], S_XY[h], in_plane(o))
        sent.append((r_xy[h].at[pl.ds(0, PLANE - 1)], S_XY[h]))
        r_xy[h][plane] = both_cores(STARTS[h] + plane * rows, rows)

    receive(cp_buf.at[pl.ds(0, 4)], S_CH)

    def stack_sides(f, carry):
        stack_cot(cp_buf[f, 0].astype(F32) * above, f, 0)
        stack_cot(cp_buf[f, 3].astype(F32) * below, f, 3)
        return carry

    lax.fori_loop(0, FR, stack_sides, 0)

    def stack_next(f, carry):
        for r in range(RB + 2):
            edge = above if r == 0 else below if r == RB + 1 else 1.0
            stack_cot(cp_buf[f, r].astype(F32) * (same_next * edge), f, r)
        return carry

    lax.fori_loop(FR, FR + 2, stack_next, 0)

    acc[...] = jnp.zeros_like(acc)

    def contract(window, k):
        return lax.dot_general(
            window, k, (((1,), (1,)), ((), ())), preferred_element_type=F32
        )

    def adjoint_tap(t, carry):
        dt, dr = lax.div(t, 3), lax.rem(t, 3)
        window = cot_st[pl.ds(2 - dt, FR), pl.ds(2 - dr, RB)].reshape(FR * RB * W, 3 * C)
        acc[...] += contract(window, wcat[t])
        return carry

    lax.fori_loop(0, 9, adjoint_tap, 0)

    def front_tap(dr, carry):
        zero = cot_st[0, pl.ds(2 - dr, RB)].reshape(RB * W, 3 * C)
        one = cot_st[1, pl.ds(2 - dr, RB)].reshape(RB * W, 3 * C)
        front = contract(zero, wcat[dr]) + contract(one, wcat[dr]) + contract(zero, wcat[dr + 3])
        acc[0:RB * W] += starts * front
        return carry

    lax.fori_loop(0, 3, front_tap, 0)

    def pre_grads(j, sums):
        at = pl.ds(pl.multiple_of(j * W, W), W)
        normed = (frames[0, j // RB, j % RB].astype(F32) - mean) * inverse_std
        lifted = normed * gain_row + shift_row
        s = 1.0 / (1.0 + jnp.exp(-lifted))
        pre = acc[at] * s * (1.0 + lifted * (1.0 - s))
        acc[at] = pre
        return sums[0] + rows_sum(pre), sums[1] + rows_sum(pre * normed)

    zero = jnp.zeros((8, C), F32)
    shift_terms, gain_terms = lax.fori_loop(0, FR * RB, pre_grads, (zero, zero))
    shift_terms = jnp.sum(shift_terms, axis=0, keepdims=True)
    gain_terms = jnp.sum(gain_terms, axis=0, keepdims=True)
    block = jnp.concatenate([shift_terms, gain_terms, bias_terms, jnp.zeros((5, C), F32)], axis=0)
    q1_src[...] = block
    q1[plane] = block
    for o in PLANE_OFFS:
        push(q1_src, q1.at[plane], S_Q1, in_plane(o))

    sent.append((q1.at[pl.ds(0, PLANE - 1)], S_Q1))

    def add_up(ref, count):
        total = ref[0].astype(F32)
        for k in range(1, count):
            total = total + ref[k].astype(F32)
        return total.astype(BF16)

    for h in range(2):
        receive(r_xy[h].at[pl.ds(0, PLANE - 1)], S_XY[h])
        r_z[h][z] = add_up(r_xy[h], PLANE)
        for o in Z_OFFS:
            push(r_z[h].at[z], r_z[h].at[z], S_Z[h], in_line((o, 0)))
        sent.append((r_z[h].at[pl.ds(0, NZ - 1)], S_Z[h]))

    def stack_act(f, carry):
        for r in range(RB + 2):
            v = act[f, r].astype(F32)
            act_st[f, r, :, 0:C] = shifted(v, True).astype(BF16)
            act_st[f, r, :, C:2 * C] = act[f, r]
            act_st[f, r, :, 2 * C:3 * C] = shifted(v, False).astype(BF16)
        return carry

    lax.fori_loop(0, FR + 2, stack_act, 0)
    out_acc[...] = jnp.zeros_like(out_acc) + bias[...]

    def forward_tap(t, carry):
        dt, dr = lax.div(t, 3), lax.rem(t, 3)
        window = act_st[pl.ds(dt, FR), pl.ds(dr, RB)].reshape(FR * RB * W, 3 * C)
        out_acc[...] += jnp.dot(window, wt[t], preferred_element_type=F32)
        return carry

    lax.fori_loop(0, 9, forward_tap, 0)
    enc_out[0] = out_acc[...].astype(BF16).reshape(FR, RB, W, C)

    for h in range(2):
        receive(r_z[h].at[pl.ds(0, NZ - 1)], S_Z[h])
        t_xy[h][plane] = add_up(r_z[h], NZ)
        for o in PLANE_OFFS:
            push(t_xy[h].at[plane], t_xy[h].at[plane], S_GXY[h], in_plane(o))
        sent.append((t_xy[h].at[pl.ds(0, PLANE - 1)], S_GXY[h]))

    receive(q1.at[pl.ds(0, PLANE - 1)], S_Q1)
    rows = []
    bias_sum = jnp.zeros((1, C), F32)
    for a in range(NX):
        summed = q1[a * NY] + q1[a * NY + 1] + q1[a * NY + 2] + q1[a * NY + 3]
        rows.append(summed)
        bias_sum = bias_sum + summed[2:3]
    block = jnp.concatenate(
        [q[0:1] for q in rows] + [q[1:2] for q in rows] + [bias_sum, jnp.zeros((7, C), F32)], axis=0
    )
    q2_src[...] = block
    q2[line] = block
    for o in LINE_OFFS:
        push(q2_src, q2.at[line], S_Q2, in_line(o))
    sent.append((q2.at[pl.ds(0, LINE - 1)], S_Q2))

    def write(ref, h, region):
        size = min(PLANE * PARTS[h], HALF - STARTS[h])
        at = pl.multiple_of(region * HALF + STARTS[h], 64)
        wg_out[pl.ds(at, size)] = ref[h][...].reshape(PLANE * PARTS[h], C)[0:size]

    def hand_over(h):
        receive(t_xy[h].at[pl.ds(0, PLANE - 1)], S_GXY[h])
        push(t_xy[h], t_core[h], S_GCORE[h], in_line((0, 1)))
        sent.append((t_core[h], S_GCORE[h]))

    hand_over(0)

    receive(q2.at[pl.ds(0, LINE - 1)], S_Q2)
    summed = jnp.zeros((8, C), F32)
    whole = jnp.zeros((16, C), F32)
    for k in range(LINE):
        part = q2[k]
        whole = whole + part
        summed = summed + part[0:8] * masks[k]
    first_mean = group_sum(jnp.sum(summed[0:4], axis=0, keepdims=True) * gain_row) * inv_count
    second_mean = group_sum(jnp.sum(summed[4:8], axis=0, keepdims=True) * gain_row) * inv_count
    factor = 1.0 / math.sqrt(POSITIONS)
    small_out[...] = jnp.concatenate(
        [
            whole[8:9],
            jnp.sum(whole[4:8], axis=0, keepdims=True),
            jnp.sum(whole[0:4], axis=0, keepdims=True),
            jnp.zeros((5, C), F32),
        ],
        axis=0,
    ) * factor

    def frame_grads(j, carry):
        at = pl.ds(pl.multiple_of(j * W, W), W)
        normed = (frames[0, j // RB, j % RB].astype(F32) - mean) * inverse_std
        result = inverse_std * (acc[at] * gain_row - first_mean - normed * second_mean)
        fg_out[0, j // RB, j % RB] = result.astype(BF16)
        return carry

    lax.fori_loop(0, FR * RB, frame_grads, 0)

    hand_over(1)
    write(t_xy, 0, c)
    write(t_xy, 1, c)
    for h in range(2):
        receive(t_core[h], S_GCORE[h])
        write(t_core, h, 1 - c)
    finish()


def writer(enc, fg, wg, small, enc_out, fg_out, wg_out, bias_out, gain_out, shift_out, wide, sems):
    copies = [
        pltpu.make_async_copy(enc, enc_out, sems.at[0]),
        pltpu.make_async_copy(fg, fg_out, sems.at[1]),
    ]
    for copy in copies:
        copy.start()
    factor = 1.0 / math.sqrt(POSITIONS)
    part = TAP_ROWS // 3
    for k in range(3):
        at = pl.ds(k * part, part)
        wide[at] = wg[at].astype(F32) * factor
        copy = pltpu.make_async_copy(wide.at[at], wg_out.at[at], sems.at[2 + k])
        copy.start()
        copies.append(copy)
    bias_out[...] = small[0:1]
    gain_out[...] = small[1:2]
    shift_out[...] = small[2:3]
    for copy in copies:
        copy.wait()


def local(frames, cotangent, conv_weight, conv_bias, norm_gain, norm_shift, clip_ids):
    vmem = pl.BlockSpec(memory_space=pltpu.VMEM)
    hbm = pl.BlockSpec(memory_space=pltpu.HBM)
    row = jax.ShapeDtypeStruct((1, C), F32)
    operands = (
        frames,
        cotangent,
        conv_weight.reshape(9, 3 * C, C),
        conv_bias.reshape(1, C),
        norm_gain.reshape(1, C),
        norm_shift.reshape(1, C),
        clip_ids,
    )
    enc, fg, wg, small = pl.pallas_call(
        kernel,
        out_shape=(
            jax.ShapeDtypeStruct(frames.shape, BF16),
            jax.ShapeDtypeStruct(frames.shape, BF16),
            jax.ShapeDtypeStruct((TAP_ROWS, C), BF16),
            jax.ShapeDtypeStruct((8, C), F32),
        ),
        in_specs=[hbm] * 7,
        out_specs=(vmem,) * 4,
        scratch_shapes=[
            pltpu.VMEM(frames.shape, BF16),
            pltpu.VMEM(frames.shape, BF16),
            pltpu.VMEM((9, 3 * C, C), BF16),
            pltpu.VMEM((1, C), F32),
            pltpu.VMEM((1, C), F32),
            pltpu.VMEM((1, C), F32),
            pltpu.SMEM((SPANS,), jnp.int32),
            pltpu.VMEM((FR + 2, RB + 2, W, C), BF16),
            pltpu.VMEM((FR + 2, RB + 2, W, C), BF16),
            pltpu.VMEM((FR + 2, RB + 2, W, C), BF16),
            pltpu.VMEM((FR + 2, 3 * C, RB * W), BF16),
            pltpu.VMEM((FR + 2, RB + 2, W, 3 * C), BF16),
            pltpu.VMEM((FR + 2, RB + 2, W, 3 * C), BF16),
            pltpu.VMEM((9, C, 3 * C), BF16),
            pltpu.VMEM((8, C), F32),
            pltpu.VMEM((PLANE, 8, C), F32),
            pltpu.VMEM((8, C), F32),
            pltpu.VMEM((LINE, 8, C), F32),
            pltpu.VMEM((8, C), F32),
            pltpu.VMEM((PLANE, 8, C), F32),
            pltpu.VMEM((16, C), F32),
            pltpu.VMEM((LINE, 16, C), F32),
            pltpu.VMEM((LINE, 8, C), F32),
            pltpu.VMEM((NC * REGION, C), F32),
            pltpu.VMEM((REGION, C), F32),
            pltpu.VMEM((REGION, C), BF16),
            *[pltpu.VMEM((PLANE, rows, C), BF16) for rows in PARTS],
            *[pltpu.VMEM((NZ, rows, C), BF16) for rows in PARTS],
            *[pltpu.VMEM((PLANE, rows, C), BF16) for rows in PARTS],
            *[pltpu.VMEM((PLANE, rows, C), BF16) for rows in PARTS],
            pltpu.VMEM((FR * RB * W, C), F32),
            pltpu.VMEM((FR * RB * W, C), F32),
            pltpu.SemaphoreType.DMA((SEMS,)),
            pltpu.SemaphoreType.DMA((SEMS,)),
            pltpu.SemaphoreType.DMA((7,)),
        ],
        compiler_params=pltpu.CompilerParams(
            collective_id=0, has_side_effects=True, vmem_limit_bytes=48 * 2**20
        ),
        cost_estimate=pl.CostEstimate(flops=3 * 10**9, bytes_accessed=4 * 10**6, transcendentals=10**6),
        name="block",
    )(*(pltpu.with_memory_space_constraint(v, pltpu.HBM) for v in operands))
    enc, fg, wg, bias, gain, shift = pl.pallas_call(
        writer,
        out_shape=(
            jax.ShapeDtypeStruct(frames.shape, BF16),
            jax.ShapeDtypeStruct(frames.shape, BF16),
            jax.ShapeDtypeStruct((TAP_ROWS, C), F32),
            row, row, row,
        ),
        in_specs=[vmem] * 4,
        out_specs=(hbm,) * 3 + (vmem,) * 3,
        scratch_shapes=[pltpu.VMEM((TAP_ROWS, C), F32), pltpu.SemaphoreType.DMA((5,))],
        compiler_params=pltpu.CompilerParams(vmem_limit_bytes=32 * 2**20),
        name="writer",
    )(enc, fg, wg, small)
    return (
        enc, fg, wg.reshape(conv_weight.shape),
        bias.reshape(C), gain.reshape(C), shift.reshape(C),
    )


def solution(mesh):
    placed = (P("span", None, "space", None, None),) * 2 + (P(),) * 5
    return jax.shard_map(
        local,
        mesh=mesh,
        in_specs=placed,
        out_specs=(P("span", None, "space", None, None),) * 2 + (P(),) * 4,
        check_vma=False,
    )
```

```python
import math

import jax
import jax.numpy as jnp
from jax import lax
from jax.experimental import pallas as pl
from jax.experimental.pallas import tpu as pltpu
from jax.sharding import PartitionSpec as P

MESH = pl.DeviceIdType.MESH
F32 = jnp.float32
BF16 = jnp.bfloat16

NX, NY, NZ, NC = 4, 4, 8, 2
SPANS = NX * NZ * NC
PLANE = NX * NY
LINE = NZ * NC
C = 128
PER_GROUP = 4
FR = 4
RB = 2
W = 128
EPSILON = 1e-06
POSITIONS = SPANS * FR * RB * NY * W
PER_DEVICE = FR * RB * W * PER_GROUP
PER_SPAN = PER_DEVICE * NY
TAP_ROWS = 27 * C
HALF = TAP_ROWS // 2
CHUNK_P, CHUNK_Q = 80, 64
ROWS_P, ROWS_Q = PLANE * CHUNK_P, NZ * CHUNK_Q
REGION = ROWS_P + ROWS_Q

(S_P1, S_P2, S_FH, S_CH, S_CORE, S_Q1, S_Q2) = range(7)
(S_PA, S_PB, S_PC, S_PD, S_QA, S_QB, S_QC, S_QD) = range(7, 15)
SEMS = 15


def group_sum(v):
    lane = lax.broadcasted_iota(jnp.int32, v.shape, 1)
    pair = v + jnp.where(lane % 2 == 0, pltpu.roll(v, 127, axis=1), pltpu.roll(v, 1, axis=1))
    return pair + jnp.where(lane % 4 < 2, pltpu.roll(pair, 126, axis=1), pltpu.roll(pair, 2, axis=1))


def distance(d, n):
    return min(d, n - d)


PLANE_OFFS = sorted(
    [(a, b) for a in range(NX) for b in range(NY) if (a, b) != (0, 0)],
    key=lambda o: -(distance(o[0], NX) + distance(o[1], NY)),
)
LINE_OFFS = sorted(
    [(a, b) for a in range(NZ) for b in range(NC) if (a, b) != (0, 0)],
    key=lambda o: -(4 * distance(o[0], NZ) + o[1]),
)
Z_OFFS = sorted(range(1, NZ), key=lambda o: -distance(o, NZ))


def wait_for(ref, sem):
    pltpu.make_async_copy(ref, ref, sem).wait()


def shifted(v, back):
    row = lax.broadcasted_iota(jnp.int32, v.shape, 0)
    if back:
        return jnp.where(row == 0, 0.0, pltpu.roll(v, 1, axis=0))
    return jnp.where(row == W - 1, 0.0, pltpu.roll(v, W - 1, axis=0))


def rows_sum(v):
    return jnp.sum(v.reshape(W // 8, 8, C), axis=0)


def kernel(
    frames_hbm, cot_hbm, wt_hbm, bias_hbm, gain_hbm, shift_hbm, clip_hbm,
    enc_out, fg_out, wg_out, small_out,
    frames, cot, wt, bias, gain, shift, clip, fp_buf, cp_buf, act, act_t, act_st, cot_st, wcat,
    p1_src, p1, p2_src, p2, q1_src, q1, q2_src, q2, masks,
    grads, r_core, s_xy, pa, pb, pc, pd, qa, qb, qc, qd, acc, out_acc,
    send, recv, load,
):
    arrays = (
        (frames_hbm, frames), (clip_hbm, clip), (cot_hbm, cot), (gain_hbm, gain),
        (shift_hbm, shift), (bias_hbm, bias), (wt_hbm, wt),
    )
    loads = [pltpu.make_async_copy(a, b, load.at[i]) for i, (a, b) in enumerate(arrays)]
    loads[0].start()
    sent, arrived = [], set()

    def receive(ref, which):
        wait_for(ref, recv.at[which])
        arrived.add(which)

    def finish():
        for ref, which in sent:
            wait_for(ref, send.at[which])
            if which not in arrived:
                receive(ref, which)

    span = lax.axis_index("span")
    y = lax.axis_index("space")
    x = lax.div(span, LINE)
    line = lax.rem(span, LINE)
    z = lax.div(line, NC)
    c = lax.rem(span, NC)
    plane = x * NY + y

    def in_plane(o):
        return (lax.rem(x + o[0], NX) * LINE + line, lax.rem(y + o[1], NY))

    def in_line(o):
        return (x * LINE + lax.rem(z + o[0], NZ) * NC + lax.rem(c + o[1], NC), y)

    def beside(ds, dy):
        return (lax.rem(span + ds + SPANS, SPANS), lax.rem(y + dy + NY, NY))

    def push(src, dst, which, device):
        pltpu.make_async_remote_copy(
            src_ref=src, dst_ref=dst, send_sem=send.at[which], recv_sem=recv.at[which],
            device_id=device, device_id_type=MESH,
        ).start()

    barrier = pltpu.get_barrier_semaphore()
    partners = [in_plane(o) for o in PLANE_OFFS] + [in_line(o) for o in LINE_OFFS]
    partners += [beside(ds, dy) for ds in (-1, 1) for dy in (-1, 0, 1)]
    far = [distance(a, NX) + distance(b, NY) for a, b in PLANE_OFFS]
    far += [distance(a, NZ) + b for a, b in LINE_OFFS] + [2.5, 1.5, 2.5] * 2
    partners = [device for _, device in sorted(zip(far, partners), key=lambda p: -p[0])]
    for device in partners:
        pl.semaphore_signal(barrier, inc=1, device_id=device, device_id_type=MESH)

    for copy in loads[1:]:
        copy.start()

    loads[0].wait()

    def add_rows(j, total):
        return total + rows_sum(frames[0, j // RB, j % RB].astype(F32))

    total = lax.fori_loop(0, FR * RB, add_rows, jnp.zeros((8, C), F32))
    mean_here = group_sum(jnp.sum(total, axis=0, keepdims=True)) * (1.0 / PER_DEVICE)

    def add_squares(j, total):
        v = frames[0, j // RB, j % RB].astype(F32) - mean_here
        return total + rows_sum(v * v)

    total = lax.fori_loop(0, FR * RB, add_squares, jnp.zeros((8, C), F32))
    squares_here = group_sum(jnp.sum(total, axis=0, keepdims=True))
    block = jnp.concatenate([mean_here, squares_here, jnp.zeros((6, C), F32)], axis=0)
    p1_src[...] = block
    p1[plane] = block

    pl.semaphore_wait(barrier, len(partners))
    for o in PLANE_OFFS:
        push(p1_src, p1.at[plane], S_P1, in_plane(o))
    sent.append((p1.at[pl.ds(0, PLANE - 1)], S_P1))
    push(frames.at[0, :, 1], fp_buf.at[pl.ds(2, FR), 0], S_FH, beside(0, 1))
    push(frames.at[0, :, 0], fp_buf.at[pl.ds(2, FR), 3], S_FH, beside(0, -1))
    push(frames.at[0, pl.ds(2, 2)], fp_buf.at[pl.ds(0, 2), pl.ds(1, RB)], S_FH, beside(1, 0))
    push(frames.at[0, pl.ds(2, 2), 1], fp_buf.at[pl.ds(0, 2), 0], S_FH, beside(1, 1))
    push(frames.at[0, pl.ds(2, 2), 0], fp_buf.at[pl.ds(0, 2), 3], S_FH, beside(1, -1))

    sent.append((fp_buf.at[pl.ds(0, 4)], S_FH))
    for copy in loads[1:]:
        copy.wait()

    for r in range(NC):
        grads[r * REGION + HALF:(r + 1) * REGION] = jnp.zeros((REGION - HALF, C), F32)
    r_core[HALF:REGION] = jnp.zeros((REGION - HALF, C), F32)

    own = clip[span]
    before = clip[lax.rem(span + SPANS - 1, SPANS)]
    after = clip[lax.rem(span + 1, SPANS)]
    starts = jnp.where((span == 0) | (before != own), 1.0, 0.0).astype(F32)
    same_next = jnp.where((span < SPANS - 1) & (after == own), 1.0, 0.0).astype(F32)
    above = jnp.where(y > 0, 1.0, 0.0).astype(F32)
    below = jnp.where(y < NY - 1, 1.0, 0.0).astype(F32)

    sub = lax.broadcasted_iota(jnp.int32, (8, C), 0)

    def fill_masks(k, count):
        block = jnp.zeros((8, C), F32)
        for a in range(NX):
            member = jnp.where(clip[a * LINE + k] == own, 1.0, 0.0).astype(F32)
            block = block + jnp.where(sub % 4 == a, member, 0.0)
            count = count + member
        masks[k] = block
        return count

    spans_here = lax.fori_loop(0, LINE, fill_masks, jnp.float32(0.0))
    spans_row = jnp.zeros((1, C), F32) + spans_here
    inv_count = 1.0 / (spans_row * PER_SPAN)

    def stack_cot(v, f, r):
        cot_st[f, r, :, 0:C] = shifted(v, False).astype(BF16)
        cot_st[f, r, :, C:2 * C] = v.astype(BF16)
        cot_st[f, r, :, 2 * C:3 * C] = shifted(v, True).astype(BF16)

    def stack_own(f, total):
        for r in range(RB):
            v = cot[0, f, r].astype(F32)
            total = total + rows_sum(v)
            stack_cot(v, f, r + 1)
            fp_buf[f + 2, r + 1] = frames[0, f, r]
        return total

    bias_terms = lax.fori_loop(0, FR, stack_own, jnp.zeros((8, C), F32))
    bias_terms = jnp.sum(bias_terms, axis=0, keepdims=True)

    receive(p1.at[pl.ds(0, PLANE - 1)], S_P1)
    mean_rows, square_rows = [], []
    for a in range(NX):
        parts = [p1[a * NY + b] for b in range(NY)]
        summed = parts[0] + parts[1] + parts[2] + parts[3]
        mean = summed[0:1] * (1.0 / NY)
        spread = sum((q[0:1] - mean) * (q[0:1] - mean) for q in parts)
        mean_rows.append(mean)
        square_rows.append(summed[1:2] + PER_DEVICE * spread)
    block = jnp.concatenate(mean_rows + square_rows, axis=0)
    p2_src[...] = block
    p2[line] = block
    for o in LINE_OFFS:
        push(p2_src, p2.at[line], S_P2, in_line(o))
    sent.append((p2.at[pl.ds(0, LINE - 1)], S_P2))
    push(cot.at[0, :, 1], cp_buf.at[pl.ds(0, FR), 0], S_CH, beside(0, 1))
    push(cot.at[0, :, 0], cp_buf.at[pl.ds(0, FR), 3], S_CH, beside(0, -1))
    push(cot.at[0, pl.ds(0, 2)], cp_buf.at[pl.ds(4, 2), pl.ds(1, RB)], S_CH, beside(-1, 0))
    push(cot.at[0, pl.ds(0, 2), 1], cp_buf.at[pl.ds(4, 2), 0], S_CH, beside(-1, 1))
    push(cot.at[0, pl.ds(0, 2), 0], cp_buf.at[pl.ds(4, 2), 3], S_CH, beside(-1, -1))

    sent.append((cp_buf.at[pl.ds(0, 4)], S_CH))

    def widen(t, carry):
        for ds in range(3):
            wcat[t, :, ds * C:(ds + 1) * C] = wt[t, pl.ds(ds * C, C)]
        return carry

    lax.fori_loop(0, 9, widen, 0)

    receive(fp_buf.at[pl.ds(0, 4)], S_FH)

    def carry_rows(r, carry):
        first = fp_buf[2, r].astype(F32) * starts
        for f in range(2):
            fp_buf[f, r] = (first + fp_buf[f, r].astype(F32) * (1.0 - starts)).astype(BF16)
        return carry

    lax.fori_loop(0, RB + 2, carry_rows, 0)

    receive(p2.at[pl.ds(0, LINE - 1)], S_P2)
    summed = jnp.zeros((8, C), F32)
    for k in range(LINE):
        summed = summed + p2[k] * masks[k]
    mean = jnp.sum(summed[0:4], axis=0, keepdims=True) / spans_row
    squares = jnp.sum(summed[4:8], axis=0, keepdims=True)
    spread = jnp.zeros((8, C), F32)
    for k in range(LINE):
        off = p2[k] - mean
        spread = spread + off * off * masks[k]
    squares = squares + PER_SPAN * jnp.sum(spread[0:4], axis=0, keepdims=True)
    inverse_std = lax.rsqrt(squares * inv_count + EPSILON)
    gain_row = gain[...]
    shift_row = shift[...]
    lift = inverse_std * gain_row

    def activate(f, carry):
        for r in range(RB + 2):
            lifted = (fp_buf[f, r].astype(F32) - mean) * lift + shift_row
            a = lifted / (1.0 + jnp.exp(-lifted))
            if r == 0:
                a = a * above
            if r == RB + 1:
                a = a * below
            act[f, r] = a.astype(BF16)
            flat = a.T.astype(BF16)
            for k in range(RB):
                dr = r - k
                if 0 <= dr < 3:
                    act_t[f, dr * C:(dr + 1) * C, k * W:(k + 1) * W] = flat
        return carry

    lax.fori_loop(0, FR + 2, activate, 0)

    cotangents = cot_st[0:FR, 1:1 + RB].reshape(FR * RB * W, 3 * C)
    for k in range(3):
        t = c * k + (1 - c) * (2 - k)
        left = jnp.concatenate([act_t[t + f] for f in range(FR)], axis=1)
        g = jnp.dot(left, cotangents, preferred_element_type=F32)
        for b in range(9):
            dr, ds = b // 3, b % 3
            piece = g[dr * C:(dr + 1) * C, ds * C:(ds + 1) * C]
            if k != 1:
                at = pl.multiple_of(t * (9 * C + 32) + b * C, 64)
                grads[pl.ds(at, C)] = piece
            elif b != 4:
                at = (9 + b) * C + (REGION - HALF if b > 4 else 0)
                grads[at:at + C] = piece
            else:
                grads[HALF - 64:HALF] = piece[0:64]
                grads[REGION:REGION + 64] = piece[64:128]
        if k < 2:
            size = (9 * C, HALF - 9 * C)[k]
            source = ((1 - c) * 2 * (9 * C + 32), c * 9 * C + (1 - c) * REGION)[k]
            target = ((1 - c) * (HALF - 9 * C), c * 9 * C)[k]
            push(
                grads.at[pl.ds(pl.multiple_of(source, 64), size)],
                r_core.at[pl.ds(pl.multiple_of(target, 64), size)],
                S_CORE, in_line((0, 1)),
            )
    sent.append((r_core.at[pl.ds(0, HALF)], S_CORE))
    receive(r_core.at[pl.ds(0, HALF)], S_CORE)
    mine = c * REGION

    def both_cores(at, rows):
        a = grads[pl.ds(pl.multiple_of(mine + at, 16), rows)]
        return (a + r_core[pl.ds(pl.multiple_of(at, 16), rows)]).astype(BF16)

    for o in PLANE_OFFS:
        px, py = lax.rem(x + o[0], NX), lax.rem(y + o[1], NY)
        at = pl.multiple_of((px * NY + py) * CHUNK_P, 16)
        s_xy[pl.ds(at, CHUNK_P)] = both_cores(at, CHUNK_P)
        push(s_xy.at[pl.ds(at, CHUNK_P)], pa.at[plane], S_PA, in_plane(o))
    for o in Z_OFFS:
        at = pl.multiple_of(ROWS_P + lax.rem(z + o, NZ) * CHUNK_Q, 16)
        s_xy[pl.ds(at, CHUNK_Q)] = both_cores(at, CHUNK_Q)
        push(s_xy.at[pl.ds(at, CHUNK_Q)], qa.at[z], S_QA, in_line((o, 0)))
    sent.append((pa.at[pl.ds(0, PLANE - 1)], S_PA))
    sent.append((qa.at[pl.ds(0, NZ - 1)], S_QA))
    pa[plane] = both_cores(plane * CHUNK_P, CHUNK_P)
    qa[z] = both_cores(ROWS_P + z * CHUNK_Q, CHUNK_Q)

    receive(cp_buf.at[pl.ds(0, 4)], S_CH)

    def stack_sides(f, carry):
        stack_cot(cp_buf[f, 0].astype(F32) * above, f, 0)
        stack_cot(cp_buf[f, 3].astype(F32) * below, f, 3)
        return carry

    lax.fori_loop(0, FR, stack_sides, 0)

    def stack_next(f, carry):
        for r in range(RB + 2):
            edge = above if r == 0 else below if r == RB + 1 else 1.0
            stack_cot(cp_buf[f, r].astype(F32) * (same_next * edge), f, r)
        return carry

    lax.fori_loop(FR, FR + 2, stack_next, 0)

    acc[...] = jnp.zeros_like(acc)

    def contract(window, k):
        return lax.dot_general(
            window, k, (((1,), (1,)), ((), ())), preferred_element_type=F32
        )

    def adjoint_tap(t, carry):
        dt, dr = lax.div(t, 3), lax.rem(t, 3)
        window = cot_st[pl.ds(2 - dt, FR), pl.ds(2 - dr, RB)].reshape(FR * RB * W, 3 * C)
        acc[...] += contract(window, wcat[t])
        return carry

    lax.fori_loop(0, 9, adjoint_tap, 0)

    def front_tap(dr, carry):
        zero = cot_st[0, pl.ds(2 - dr, RB)].reshape(RB * W, 3 * C)
        one = cot_st[1, pl.ds(2 - dr, RB)].reshape(RB * W, 3 * C)
        front = contract(zero, wcat[dr]) + contract(one, wcat[dr]) + contract(zero, wcat[dr + 3])
        acc[0:RB * W] += starts * front
        return carry

    lax.fori_loop(0, 3, front_tap, 0)

    def pre_grads(j, sums):
        at = pl.ds(pl.multiple_of(j * W, W), W)
        normed = (frames[0, j // RB, j % RB].astype(F32) - mean) * inverse_std
        lifted = normed * gain_row + shift_row
        s = 1.0 / (1.0 + jnp.exp(-lifted))
        pre = acc[at] * s * (1.0 + lifted * (1.0 - s))
        acc[at] = pre
        return sums[0] + rows_sum(pre), sums[1] + rows_sum(pre * normed)

    zero = jnp.zeros((8, C), F32)
    shift_terms, gain_terms = lax.fori_loop(0, FR * RB, pre_grads, (zero, zero))
    shift_terms = jnp.sum(shift_terms, axis=0, keepdims=True)
    gain_terms = jnp.sum(gain_terms, axis=0, keepdims=True)
    block = jnp.concatenate([shift_terms, gain_terms, bias_terms, jnp.zeros((5, C), F32)], axis=0)
    q1_src[...] = block
    q1[plane] = block
    for o in PLANE_OFFS:
        push(q1_src, q1.at[plane], S_Q1, in_plane(o))

    sent.append((q1.at[pl.ds(0, PLANE - 1)], S_Q1))

    def stack_act(f, carry):
        for r in range(RB + 2):
            v = act[f, r].astype(F32)
            act_st[f, r, :, 0:C] = shifted(v, True).astype(BF16)
            act_st[f, r, :, C:2 * C] = act[f, r]
            act_st[f, r, :, 2 * C:3 * C] = shifted(v, False).astype(BF16)
        return carry

    lax.fori_loop(0, FR + 2, stack_act, 0)

    def add_up(ref, count):
        total = ref[0].astype(F32)
        for k in range(1, count):
            total = total + ref[k].astype(F32)
        return total.astype(BF16)

    receive(qa.at[pl.ds(0, NZ - 1)], S_QA)
    qb[plane] = add_up(qa, NZ)
    for o in PLANE_OFFS:
        push(qb.at[plane], qb.at[plane], S_QB, in_plane(o))
    sent.append((qb.at[pl.ds(0, PLANE - 1)], S_QB))
    receive(pa.at[pl.ds(0, PLANE - 1)], S_PA)
    pb[z] = add_up(pa, PLANE)
    for o in Z_OFFS:
        push(pb.at[z], pb.at[z], S_PB, in_line((o, 0)))
    sent.append((pb.at[pl.ds(0, NZ - 1)], S_PB))

    out_acc[...] = jnp.zeros_like(out_acc) + bias[...]

    def forward_tap(t, carry):
        dt, dr = lax.div(t, 3), lax.rem(t, 3)
        window = act_st[pl.ds(dt, FR), pl.ds(dr, RB)].reshape(FR * RB * W, 3 * C)
        out_acc[...] += jnp.dot(window, wt[t], preferred_element_type=F32)
        return carry

    lax.fori_loop(0, 5, forward_tap, 0)

    receive(q1.at[pl.ds(0, PLANE - 1)], S_Q1)
    rows = []
    bias_sum = jnp.zeros((1, C), F32)
    for a in range(NX):
        summed = q1[a * NY] + q1[a * NY + 1] + q1[a * NY + 2] + q1[a * NY + 3]
        rows.append(summed)
        bias_sum = bias_sum + summed[2:3]
    block = jnp.concatenate(
        [q[0:1] for q in rows] + [q[1:2] for q in rows] + [bias_sum, jnp.zeros((7, C), F32)], axis=0
    )
    q2_src[...] = block
    q2[line] = block
    for o in LINE_OFFS:
        push(q2_src, q2.at[line], S_Q2, in_line(o))
    sent.append((q2.at[pl.ds(0, LINE - 1)], S_Q2))
    lax.fori_loop(5, 9, forward_tap, 0)
    enc_out[0] = out_acc[...].astype(BF16).reshape(FR, RB, W, C)

    receive(pb.at[pl.ds(0, NZ - 1)], S_PB)
    pc[plane] = add_up(pb, NZ)
    for o in PLANE_OFFS:
        push(pc.at[plane], pc.at[plane], S_PC, in_plane(o))
    sent.append((pc.at[pl.ds(0, PLANE - 1)], S_PC))
    receive(qb.at[pl.ds(0, PLANE - 1)], S_QB)
    qc[z] = add_up(qb, PLANE)
    for o in Z_OFFS:
        push(qc.at[z], qc.at[z], S_QC, in_line((o, 0)))
    sent.append((qc.at[pl.ds(0, NZ - 1)], S_QC))


    def write(ref_p, ref_q, region):
        at = pl.multiple_of(region * HALF, 64)
        wg_out[pl.ds(at, ROWS_P)] = ref_p[...].reshape(ROWS_P, C)
        at = pl.multiple_of(region * HALF + ROWS_P, 64)
        wg_out[pl.ds(at, HALF - ROWS_P)] = ref_q[...].reshape(ROWS_Q, C)[0:HALF - ROWS_P]


    receive(q2.at[pl.ds(0, LINE - 1)], S_Q2)
    summed = jnp.zeros((8, C), F32)
    whole = jnp.zeros((16, C), F32)
    for k in range(LINE):
        part = q2[k]
        whole = whole + part
        summed = summed + part[0:8] * masks[k]
    first_mean = group_sum(jnp.sum(summed[0:4], axis=0, keepdims=True) * gain_row) * inv_count
    second_mean = group_sum(jnp.sum(summed[4:8], axis=0, keepdims=True) * gain_row) * inv_count
    factor = 1.0 / math.sqrt(POSITIONS)
    small_out[...] = jnp.concatenate(
        [
            whole[8:9],
            jnp.sum(whole[4:8], axis=0, keepdims=True),
            jnp.sum(whole[0:4], axis=0, keepdims=True),
            jnp.zeros((5, C), F32),
        ],
        axis=0,
    ) * factor

    def frame_grads(j, carry):
        at = pl.ds(pl.multiple_of(j * W, W), W)
        normed = (frames[0, j // RB, j % RB].astype(F32) - mean) * inverse_std
        result = inverse_std * (acc[at] * gain_row - first_mean - normed * second_mean)
        fg_out[0, j // RB, j % RB] = result.astype(BF16)
        return carry

    lax.fori_loop(0, FR * RB, frame_grads, 0)

    receive(qc.at[pl.ds(0, NZ - 1)], S_QC)
    push(qc, qd, S_QD, in_line((0, 1)))
    sent.append((qd, S_QD))
    receive(pc.at[pl.ds(0, PLANE - 1)], S_PC)
    push(pc, pd, S_PD, in_line((0, 1)))
    sent.append((pd, S_PD))
    write(pc, qc, c)
    receive(qd, S_QD)
    receive(pd, S_PD)
    write(pd, qd, 1 - c)
    finish()


def writer(enc, fg, wg, small, enc_out, fg_out, wg_out, bias_out, gain_out, shift_out, wide, sems):
    copies = [
        pltpu.make_async_copy(enc, enc_out, sems.at[0]),
        pltpu.make_async_copy(fg, fg_out, sems.at[1]),
    ]
    for copy in copies:
        copy.start()
    factor = 1.0 / math.sqrt(POSITIONS)
    part = TAP_ROWS // 3
    for k in range(3):
        at = pl.ds(k * part, part)
        wide[at] = wg[at].astype(F32) * factor
        copy = pltpu.make_async_copy(wide.at[at], wg_out.at[at], sems.at[2 + k])
        copy.start()
        copies.append(copy)
    bias_out[...] = small[0:1]
    gain_out[...] = small[1:2]
    shift_out[...] = small[2:3]
    for copy in copies:
        copy.wait()


def local(frames, cotangent, conv_weight, conv_bias, norm_gain, norm_shift, clip_ids):
    vmem = pl.BlockSpec(memory_space=pltpu.VMEM)
    hbm = pl.BlockSpec(memory_space=pltpu.HBM)
    row = jax.ShapeDtypeStruct((1, C), F32)
    operands = (
        frames,
        cotangent,
        conv_weight.reshape(9, 3 * C, C),
        conv_bias.reshape(1, C),
        norm_gain.reshape(1, C),
        norm_shift.reshape(1, C),
        clip_ids,
    )
    enc, fg, wg, small = pl.pallas_call(
        kernel,
        out_shape=(
            jax.ShapeDtypeStruct(frames.shape, BF16),
            jax.ShapeDtypeStruct(frames.shape, BF16),
            jax.ShapeDtypeStruct((TAP_ROWS, C), BF16),
            jax.ShapeDtypeStruct((8, C), F32),
        ),
        in_specs=[hbm] * 7,
        out_specs=(vmem,) * 4,
        scratch_shapes=[
            pltpu.VMEM(frames.shape, BF16),
            pltpu.VMEM(frames.shape, BF16),
            pltpu.VMEM((9, 3 * C, C), BF16),
            pltpu.VMEM((1, C), F32),
            pltpu.VMEM((1, C), F32),
            pltpu.VMEM((1, C), F32),
            pltpu.SMEM((SPANS,), jnp.int32),
            pltpu.VMEM((FR + 2, RB + 2, W, C), BF16),
            pltpu.VMEM((FR + 2, RB + 2, W, C), BF16),
            pltpu.VMEM((FR + 2, RB + 2, W, C), BF16),
            pltpu.VMEM((FR + 2, 3 * C, RB * W), BF16),
            pltpu.VMEM((FR + 2, RB + 2, W, 3 * C), BF16),
            pltpu.VMEM((FR + 2, RB + 2, W, 3 * C), BF16),
            pltpu.VMEM((9, C, 3 * C), BF16),
            pltpu.VMEM((8, C), F32),
            pltpu.VMEM((PLANE, 8, C), F32),
            pltpu.VMEM((8, C), F32),
            pltpu.VMEM((LINE, 8, C), F32),
            pltpu.VMEM((8, C), F32),
            pltpu.VMEM((PLANE, 8, C), F32),
            pltpu.VMEM((16, C), F32),
            pltpu.VMEM((LINE, 16, C), F32),
            pltpu.VMEM((LINE, 8, C), F32),
            pltpu.VMEM((NC * REGION, C), F32),
            pltpu.VMEM((REGION, C), F32),
            pltpu.VMEM((REGION, C), BF16),
            pltpu.VMEM((PLANE, CHUNK_P, C), BF16),
            pltpu.VMEM((NZ, CHUNK_P, C), BF16),
            pltpu.VMEM((PLANE, CHUNK_P, C), BF16),
            pltpu.VMEM((PLANE, CHUNK_P, C), BF16),
            pltpu.VMEM((NZ, CHUNK_Q, C), BF16),
            pltpu.VMEM((PLANE, CHUNK_Q, C), BF16),
            pltpu.VMEM((NZ, CHUNK_Q, C), BF16),
            pltpu.VMEM((NZ, CHUNK_Q, C), BF16),
            pltpu.VMEM((FR * RB * W, C), F32),
            pltpu.VMEM((FR * RB * W, C), F32),
            pltpu.SemaphoreType.DMA((SEMS,)),
            pltpu.SemaphoreType.DMA((SEMS,)),
            pltpu.SemaphoreType.DMA((7,)),
        ],
        compiler_params=pltpu.CompilerParams(
            collective_id=0, has_side_effects=True, vmem_limit_bytes=48 * 2**20
        ),
        cost_estimate=pl.CostEstimate(flops=3 * 10**9, bytes_accessed=4 * 10**6, transcendentals=10**6),
        name="block",
    )(*(pltpu.with_memory_space_constraint(v, pltpu.HBM) for v in operands))
    enc, fg, wg, bias, gain, shift = pl.pallas_call(
        writer,
        out_shape=(
            jax.ShapeDtypeStruct(frames.shape, BF16),
            jax.ShapeDtypeStruct(frames.shape, BF16),
            jax.ShapeDtypeStruct((TAP_ROWS, C), F32),
            row, row, row,
        ),
        in_specs=[vmem] * 4,
        out_specs=(hbm,) * 3 + (vmem,) * 3,
        scratch_shapes=[pltpu.VMEM((TAP_ROWS, C), F32), pltpu.SemaphoreType.DMA((5,))],
        compiler_params=pltpu.CompilerParams(vmem_limit_bytes=32 * 2**20),
        name="writer",
    )(enc, fg, wg, small)
    return (
        enc, fg, wg.reshape(conv_weight.shape),
        bias.reshape(C), gain.reshape(C), shift.reshape(C),
    )


def solution(mesh):
    placed = (P("span", None, "space", None, None),) * 2 + (P(),) * 5
    return jax.shard_map(
        local,
        mesh=mesh,
        in_specs=placed,
        out_specs=(P("span", None, "space", None, None),) * 2 + (P(),) * 4,
        check_vma=False,
    )
```

```python
import math

import jax
import jax.numpy as jnp
from jax import lax
from jax.experimental import pallas as pl
from jax.experimental.pallas import tpu as pltpu
from jax.sharding import PartitionSpec as P

MESH = pl.DeviceIdType.MESH
F32 = jnp.float32
BF16 = jnp.bfloat16

NX, NY, NZ, NC = 4, 4, 8, 2
SPANS = NX * NZ * NC
PLANE = NX * NY
LINE = NZ * NC
C = 128
PER_GROUP = 4
FR = 4
RB = 2
W = 128
EPSILON = 1e-06
POSITIONS = SPANS * FR * RB * NY * W
PER_DEVICE = FR * RB * W * PER_GROUP
PER_SPAN = PER_DEVICE * NY
TAP_ROWS = 27 * C
HALF = TAP_ROWS // 2
CHUNK_P, CHUNK_Q = 80, 64
ROWS_P, ROWS_Q = PLANE * CHUNK_P, NZ * CHUNK_Q
REGION = ROWS_P + ROWS_Q

(S_P1, S_P2, S_FH, S_CH, S_CORE, S_Q1, S_Q2) = range(7)
(S_PA, S_PB, S_PC, S_PD, S_QA, S_QB, S_QC, S_QD) = range(7, 15)
SEMS = 15


def group_sum(v):
    lane = lax.broadcasted_iota(jnp.int32, v.shape, 1)
    pair = v + jnp.where(lane % 2 == 0, pltpu.roll(v, 127, axis=1), pltpu.roll(v, 1, axis=1))
    return pair + jnp.where(lane % 4 < 2, pltpu.roll(pair, 126, axis=1), pltpu.roll(pair, 2, axis=1))


def distance(d, n):
    return min(d, n - d)


PLANE_OFFS = sorted(
    [(a, b) for a in range(NX) for b in range(NY) if (a, b) != (0, 0)],
    key=lambda o: -(distance(o[0], NX) + distance(o[1], NY)),
)
LINE_OFFS = sorted(
    [(a, b) for a in range(NZ) for b in range(NC) if (a, b) != (0, 0)],
    key=lambda o: -(4 * distance(o[0], NZ) + o[1]),
)
Z_OFFS = sorted(range(1, NZ), key=lambda o: -distance(o, NZ))


def wait_for(ref, sem):
    pltpu.make_async_copy(ref, ref, sem).wait()


def shifted(v, back):
    row = lax.broadcasted_iota(jnp.int32, v.shape, 0)
    if back:
        return jnp.where(row == 0, 0.0, pltpu.roll(v, 1, axis=0))
    return jnp.where(row == W - 1, 0.0, pltpu.roll(v, W - 1, axis=0))


def rows_sum(v):
    return jnp.sum(v.reshape(W // 8, 8, C), axis=0)


def kernel(
    frames_hbm, cot_hbm, wt_hbm, bias_hbm, gain_hbm, shift_hbm, clip_hbm,
    enc_out, fg_out, wg_out, small_out,
    frames, cot, wt, bias, gain, shift, clip, fp_buf, cp_buf, act, act_t, act_st, cot_st, wcat,
    p1_src, p1, p2_src, p2, q1_src, q1, q2_src, q2, masks,
    grads, own_grads, r_core, s_xy, pa, pb, pc, pd, qa, qb, qc, qd, acc, out_acc,
    send, recv, load,
):
    arrays = (
        (frames_hbm, frames), (clip_hbm, clip), (cot_hbm, cot), (gain_hbm, gain),
        (shift_hbm, shift), (bias_hbm, bias), (wt_hbm, wt),
    )
    loads = [pltpu.make_async_copy(a, b, load.at[i]) for i, (a, b) in enumerate(arrays)]
    loads[0].start()
    sent, arrived = [], set()

    def receive(ref, which):
        wait_for(ref, recv.at[which])
        arrived.add(which)

    def finish():
        for ref, which in sent:
            wait_for(ref, send.at[which])
            if which not in arrived:
                receive(ref, which)

    span = lax.axis_index("span")
    y = lax.axis_index("space")
    x = lax.div(span, LINE)
    line = lax.rem(span, LINE)
    z = lax.div(line, NC)
    c = lax.rem(span, NC)
    plane = x * NY + y

    def in_plane(o):
        return (lax.rem(x + o[0], NX) * LINE + line, lax.rem(y + o[1], NY))

    def in_line(o):
        return (x * LINE + lax.rem(z + o[0], NZ) * NC + lax.rem(c + o[1], NC), y)

    def beside(ds, dy):
        return (lax.rem(span + ds + SPANS, SPANS), lax.rem(y + dy + NY, NY))

    def push(src, dst, which, device):
        pltpu.make_async_remote_copy(
            src_ref=src, dst_ref=dst, send_sem=send.at[which], recv_sem=recv.at[which],
            device_id=device, device_id_type=MESH,
        ).start()

    barrier = pltpu.get_barrier_semaphore()
    partners = [in_plane(o) for o in PLANE_OFFS] + [in_line(o) for o in LINE_OFFS]
    partners += [beside(ds, dy) for ds in (-1, 1) for dy in (-1, 0, 1)]
    far = [distance(a, NX) + distance(b, NY) for a, b in PLANE_OFFS]
    far += [distance(a, NZ) + b for a, b in LINE_OFFS] + [2.5, 1.5, 2.5] * 2
    partners = [device for _, device in sorted(zip(far, partners), key=lambda p: -p[0])]
    for device in partners:
        pl.semaphore_signal(barrier, inc=1, device_id=device, device_id_type=MESH)

    for copy in loads[1:]:
        copy.start()

    loads[0].wait()

    def add_rows(j, total):
        return total + rows_sum(frames[0, j // RB, j % RB].astype(F32))

    total = lax.fori_loop(0, FR * RB, add_rows, jnp.zeros((8, C), F32))
    mean_here = group_sum(jnp.sum(total, axis=0, keepdims=True)) * (1.0 / PER_DEVICE)

    def add_squares(j, total):
        v = frames[0, j // RB, j % RB].astype(F32) - mean_here
        return total + rows_sum(v * v)

    total = lax.fori_loop(0, FR * RB, add_squares, jnp.zeros((8, C), F32))
    squares_here = group_sum(jnp.sum(total, axis=0, keepdims=True))
    block = jnp.concatenate([mean_here, squares_here, jnp.zeros((6, C), F32)], axis=0)
    p1_src[...] = block
    p1[plane] = block

    pl.semaphore_wait(barrier, len(partners))
    for o in PLANE_OFFS:
        push(p1_src, p1.at[plane], S_P1, in_plane(o))
    sent.append((p1.at[pl.ds(0, PLANE - 1)], S_P1))
    push(frames.at[0, :, 1], fp_buf.at[pl.ds(2, FR), 0], S_FH, beside(0, 1))
    push(frames.at[0, :, 0], fp_buf.at[pl.ds(2, FR), 3], S_FH, beside(0, -1))
    push(frames.at[0, pl.ds(2, 2)], fp_buf.at[pl.ds(0, 2), pl.ds(1, RB)], S_FH, beside(1, 0))
    push(frames.at[0, pl.ds(2, 2), 1], fp_buf.at[pl.ds(0, 2), 0], S_FH, beside(1, 1))
    push(frames.at[0, pl.ds(2, 2), 0], fp_buf.at[pl.ds(0, 2), 3], S_FH, beside(1, -1))

    sent.append((fp_buf.at[pl.ds(0, 4)], S_FH))
    for copy in loads[1:]:
        copy.wait()

    for r in range(NC):
        own_grads[r * REGION + HALF:(r + 1) * REGION] = jnp.zeros((REGION - HALF, C), F32)
    r_core[HALF:REGION] = jnp.zeros((REGION - HALF, C), BF16)

    own = clip[span]
    before = clip[lax.rem(span + SPANS - 1, SPANS)]
    after = clip[lax.rem(span + 1, SPANS)]
    starts = jnp.where((span == 0) | (before != own), 1.0, 0.0).astype(F32)
    same_next = jnp.where((span < SPANS - 1) & (after == own), 1.0, 0.0).astype(F32)
    above = jnp.where(y > 0, 1.0, 0.0).astype(F32)
    below = jnp.where(y < NY - 1, 1.0, 0.0).astype(F32)

    sub = lax.broadcasted_iota(jnp.int32, (8, C), 0)

    def fill_masks(k, count):
        block = jnp.zeros((8, C), F32)
        for a in range(NX):
            member = jnp.where(clip[a * LINE + k] == own, 1.0, 0.0).astype(F32)
            block = block + jnp.where(sub % 4 == a, member, 0.0)
            count = count + member
        masks[k] = block
        return count

    spans_here = lax.fori_loop(0, LINE, fill_masks, jnp.float32(0.0))
    spans_row = jnp.zeros((1, C), F32) + spans_here
    inv_count = 1.0 / (spans_row * PER_SPAN)

    def stack_cot(v, f, r):
        cot_st[f, r, :, 0:C] = shifted(v, False).astype(BF16)
        cot_st[f, r, :, C:2 * C] = v.astype(BF16)
        cot_st[f, r, :, 2 * C:3 * C] = shifted(v, True).astype(BF16)

    def stack_own(f, total):
        for r in range(RB):
            v = cot[0, f, r].astype(F32)
            total = total + rows_sum(v)
            stack_cot(v, f, r + 1)
            fp_buf[f + 2, r + 1] = frames[0, f, r]
        return total

    bias_terms = lax.fori_loop(0, FR, stack_own, jnp.zeros((8, C), F32))
    bias_terms = jnp.sum(bias_terms, axis=0, keepdims=True)

    receive(p1.at[pl.ds(0, PLANE - 1)], S_P1)
    mean_rows, square_rows = [], []
    for a in range(NX):
        parts = [p1[a * NY + b] for b in range(NY)]
        summed = parts[0] + parts[1] + parts[2] + parts[3]
        mean = summed[0:1] * (1.0 / NY)
        spread = sum((q[0:1] - mean) * (q[0:1] - mean) for q in parts)
        mean_rows.append(mean)
        square_rows.append(summed[1:2] + PER_DEVICE * spread)
    block = jnp.concatenate(mean_rows + square_rows, axis=0)
    p2_src[...] = block
    p2[line] = block
    for o in LINE_OFFS:
        push(p2_src, p2.at[line], S_P2, in_line(o))
    sent.append((p2.at[pl.ds(0, LINE - 1)], S_P2))
    push(cot.at[0, :, 1], cp_buf.at[pl.ds(0, FR), 0], S_CH, beside(0, 1))
    push(cot.at[0, :, 0], cp_buf.at[pl.ds(0, FR), 3], S_CH, beside(0, -1))
    push(cot.at[0, pl.ds(0, 2)], cp_buf.at[pl.ds(4, 2), pl.ds(1, RB)], S_CH, beside(-1, 0))
    push(cot.at[0, pl.ds(0, 2), 1], cp_buf.at[pl.ds(4, 2), 0], S_CH, beside(-1, 1))
    push(cot.at[0, pl.ds(0, 2), 0], cp_buf.at[pl.ds(4, 2), 3], S_CH, beside(-1, -1))

    sent.append((cp_buf.at[pl.ds(0, 4)], S_CH))

    def widen(t, carry):
        for ds in range(3):
            wcat[t, :, ds * C:(ds + 1) * C] = wt[t, pl.ds(ds * C, C)]
        return carry

    lax.fori_loop(0, 9, widen, 0)

    receive(fp_buf.at[pl.ds(0, 4)], S_FH)

    def carry_rows(r, carry):
        first = fp_buf[2, r].astype(F32) * starts
        for f in range(2):
            fp_buf[f, r] = (first + fp_buf[f, r].astype(F32) * (1.0 - starts)).astype(BF16)
        return carry

    lax.fori_loop(0, RB + 2, carry_rows, 0)

    receive(p2.at[pl.ds(0, LINE - 1)], S_P2)
    summed = jnp.zeros((8, C), F32)
    for k in range(LINE):
        summed = summed + p2[k] * masks[k]
    mean = jnp.sum(summed[0:4], axis=0, keepdims=True) / spans_row
    squares = jnp.sum(summed[4:8], axis=0, keepdims=True)
    spread = jnp.zeros((8, C), F32)
    for k in range(LINE):
        off = p2[k] - mean
        spread = spread + off * off * masks[k]
    squares = squares + PER_SPAN * jnp.sum(spread[0:4], axis=0, keepdims=True)
    inverse_std = lax.rsqrt(squares * inv_count + EPSILON)
    gain_row = gain[...]
    shift_row = shift[...]
    lift = inverse_std * gain_row

    def activate(f, carry):
        for r in range(RB + 2):
            lifted = (fp_buf[f, r].astype(F32) - mean) * lift + shift_row
            half = 0.5 * lifted
            a = half + half * jnp.tanh(half)
            if r == 0:
                a = a * above
            if r == RB + 1:
                a = a * below
            a = a.astype(BF16)
            act[f, r] = a
            flat = a.T
            for k in range(RB):
                dr = r - k
                if 0 <= dr < 3:
                    act_t[f, dr * C:(dr + 1) * C, k * W:(k + 1) * W] = flat
        return carry

    lax.fori_loop(0, FR + 2, activate, 0)

    cotangents = cot_st[0:FR, 1:1 + RB].reshape(FR * RB * W, 3 * C)
    for k in range(3):
        t = c * k + (1 - c) * (2 - k)
        left = jnp.concatenate([act_t[t + f] for f in range(FR)], axis=1)
        g = jnp.dot(left, cotangents, preferred_element_type=F32)
        for b in range(9):
            dr, ds = b // 3, b % 3
            piece = g[dr * C:(dr + 1) * C, ds * C:(ds + 1) * C]
            for ref in ((grads,), (grads, own_grads), (own_grads,))[k]:
                part = piece.astype(ref.dtype)
                if k != 1:
                    at = pl.multiple_of(t * (9 * C + 32) + b * C, 64)
                    ref[pl.ds(at, C)] = part
                elif b != 4:
                    at = (9 + b) * C + (REGION - HALF if b > 4 else 0)
                    ref[at:at + C] = part
                else:
                    ref[HALF - 64:HALF] = part[0:64]
                    ref[REGION:REGION + 64] = part[64:128]
        if k < 2:
            size = (9 * C, HALF - 9 * C)[k]
            source = ((1 - c) * 2 * (9 * C + 32), c * 9 * C + (1 - c) * REGION)[k]
            target = ((1 - c) * (HALF - 9 * C), c * 9 * C)[k]
            push(
                grads.at[pl.ds(pl.multiple_of(source, 64), size)],
                r_core.at[pl.ds(pl.multiple_of(target, 64), size)],
                S_CORE, in_line((0, 1)),
            )
    sent.append((r_core.at[pl.ds(0, HALF)], S_CORE))
    receive(r_core.at[pl.ds(0, HALF)], S_CORE)
    mine = c * REGION

    def both_cores(at, rows):
        a = own_grads[pl.ds(pl.multiple_of(mine + at, 16), rows)]
        return (a + r_core[pl.ds(pl.multiple_of(at, 16), rows)].astype(F32)).astype(BF16)

    for o in PLANE_OFFS:
        px, py = lax.rem(x + o[0], NX), lax.rem(y + o[1], NY)
        at = pl.multiple_of((px * NY + py) * CHUNK_P, 16)
        s_xy[pl.ds(at, CHUNK_P)] = both_cores(at, CHUNK_P)
        push(s_xy.at[pl.ds(at, CHUNK_P)], pa.at[plane], S_PA, in_plane(o))
    for o in Z_OFFS:
        at = pl.multiple_of(ROWS_P + lax.rem(z + o, NZ) * CHUNK_Q, 16)
        s_xy[pl.ds(at, CHUNK_Q)] = both_cores(at, CHUNK_Q)
        push(s_xy.at[pl.ds(at, CHUNK_Q)], qa.at[z], S_QA, in_line((o, 0)))
    sent.append((pa.at[pl.ds(0, PLANE - 1)], S_PA))
    sent.append((qa.at[pl.ds(0, NZ - 1)], S_QA))
    pa[plane] = both_cores(plane * CHUNK_P, CHUNK_P)
    qa[z] = both_cores(ROWS_P + z * CHUNK_Q, CHUNK_Q)

    receive(cp_buf.at[pl.ds(0, 4)], S_CH)

    def stack_sides(f, carry):
        stack_cot(cp_buf[f, 0].astype(F32) * above, f, 0)
        stack_cot(cp_buf[f, 3].astype(F32) * below, f, 3)
        return carry

    lax.fori_loop(0, FR, stack_sides, 0)

    def stack_next(f, carry):
        for r in range(RB + 2):
            edge = above if r == 0 else below if r == RB + 1 else 1.0
            stack_cot(cp_buf[f, r].astype(F32) * (same_next * edge), f, r)
        return carry

    lax.fori_loop(FR, FR + 2, stack_next, 0)

    acc[...] = jnp.zeros_like(acc)

    def contract(window, k):
        return lax.dot_general(
            window, k, (((1,), (1,)), ((), ())), preferred_element_type=F32
        )

    def adjoint_tap(t, carry):
        dt, dr = lax.div(t, 3), lax.rem(t, 3)
        window = cot_st[pl.ds(2 - dt, FR), pl.ds(2 - dr, RB)].reshape(FR * RB * W, 3 * C)
        acc[...] += contract(window, wcat[t])
        return carry

    lax.fori_loop(0, 9, adjoint_tap, 0)

    def front_tap(dr, carry):
        zero = cot_st[0, pl.ds(2 - dr, RB)].reshape(RB * W, 3 * C)
        one = cot_st[1, pl.ds(2 - dr, RB)].reshape(RB * W, 3 * C)
        front = contract(zero, wcat[dr]) + contract(one, wcat[dr]) + contract(zero, wcat[dr + 3])
        acc[0:RB * W] += starts * front
        return carry

    lax.fori_loop(0, 3, front_tap, 0)

    def pre_grads(j, sums):
        at = pl.ds(pl.multiple_of(j * W, W), W)
        normed = (frames[0, j // RB, j % RB].astype(F32) - mean) * inverse_std
        lifted = normed * gain_row + shift_row
        s = 1.0 / (1.0 + jnp.exp(-lifted))
        pre = acc[at] * s * (1.0 + lifted * (1.0 - s))
        acc[at] = pre
        return sums[0] + rows_sum(pre), sums[1] + rows_sum(pre * normed)

    zero = jnp.zeros((8, C), F32)
    shift_terms, gain_terms = lax.fori_loop(0, FR * RB, pre_grads, (zero, zero))
    shift_terms = jnp.sum(shift_terms, axis=0, keepdims=True)
    gain_terms = jnp.sum(gain_terms, axis=0, keepdims=True)
    block = jnp.concatenate([shift_terms, gain_terms, bias_terms, jnp.zeros((5, C), F32)], axis=0)
    q1_src[...] = block
    q1[plane] = block
    for o in PLANE_OFFS:
        push(q1_src, q1.at[plane], S_Q1, in_plane(o))

    sent.append((q1.at[pl.ds(0, PLANE - 1)], S_Q1))

    def stack_act(f, carry):
        for r in range(RB + 2):
            v = act[f, r].astype(F32)
            act_st[f, r, :, 0:C] = shifted(v, True).astype(BF16)
            act_st[f, r, :, C:2 * C] = act[f, r]
            act_st[f, r, :, 2 * C:3 * C] = shifted(v, False).astype(BF16)
        return carry

    lax.fori_loop(0, FR + 2, stack_act, 0)

    def add_up(ref, count):
        total = ref[0].astype(F32)
        for k in range(1, count):
            total = total + ref[k].astype(F32)
        return total.astype(BF16)

    receive(qa.at[pl.ds(0, NZ - 1)], S_QA)
    qb[plane] = add_up(qa, NZ)
    for o in PLANE_OFFS:
        push(qb.at[plane], qb.at[plane], S_QB, in_plane(o))
    sent.append((qb.at[pl.ds(0, PLANE - 1)], S_QB))
    receive(pa.at[pl.ds(0, PLANE - 1)], S_PA)
    pb[z] = add_up(pa, PLANE)
    for o in Z_OFFS:
        push(pb.at[z], pb.at[z], S_PB, in_line((o, 0)))
    sent.append((pb.at[pl.ds(0, NZ - 1)], S_PB))

    out_acc[...] = jnp.zeros_like(out_acc) + bias[...]

    def forward_tap(t, carry):
        dt, dr = lax.div(t, 3), lax.rem(t, 3)
        window = act_st[pl.ds(dt, FR), pl.ds(dr, RB)].reshape(FR * RB * W, 3 * C)
        out_acc[...] += jnp.dot(window, wt[t], preferred_element_type=F32)
        return carry

    lax.fori_loop(0, 5, forward_tap, 0)

    receive(q1.at[pl.ds(0, PLANE - 1)], S_Q1)
    rows = []
    bias_sum = jnp.zeros((1, C), F32)
    for a in range(NX):
        summed = q1[a * NY] + q1[a * NY + 1] + q1[a * NY + 2] + q1[a * NY + 3]
        rows.append(summed)
        bias_sum = bias_sum + summed[2:3]
    block = jnp.concatenate(
        [q[0:1] for q in rows] + [q[1:2] for q in rows] + [bias_sum, jnp.zeros((7, C), F32)], axis=0
    )
    q2_src[...] = block
    q2[line] = block
    for o in LINE_OFFS:
        push(q2_src, q2.at[line], S_Q2, in_line(o))
    sent.append((q2.at[pl.ds(0, LINE - 1)], S_Q2))
    lax.fori_loop(5, 9, forward_tap, 0)
    enc_out[0] = out_acc[...].astype(BF16).reshape(FR, RB, W, C)

    receive(pb.at[pl.ds(0, NZ - 1)], S_PB)
    pc[plane] = add_up(pb, NZ)
    for o in PLANE_OFFS:
        push(pc.at[plane], pc.at[plane], S_PC, in_plane(o))
    sent.append((pc.at[pl.ds(0, PLANE - 1)], S_PC))
    receive(qb.at[pl.ds(0, PLANE - 1)], S_QB)
    qc[z] = add_up(qb, PLANE)
    for o in Z_OFFS:
        push(qc.at[z], qc.at[z], S_QC, in_line((o, 0)))
    sent.append((qc.at[pl.ds(0, NZ - 1)], S_QC))


    def write(ref_p, ref_q, region):
        at = pl.multiple_of(region * HALF, 64)
        wg_out[pl.ds(at, ROWS_P)] = ref_p[...].reshape(ROWS_P, C)
        at = pl.multiple_of(region * HALF + ROWS_P, 64)
        wg_out[pl.ds(at, HALF - ROWS_P)] = ref_q[...].reshape(ROWS_Q, C)[0:HALF - ROWS_P]


    receive(q2.at[pl.ds(0, LINE - 1)], S_Q2)
    summed = jnp.zeros((8, C), F32)
    whole = jnp.zeros((16, C), F32)
    for k in range(LINE):
        part = q2[k]
        whole = whole + part
        summed = summed + part[0:8] * masks[k]
    first_mean = group_sum(jnp.sum(summed[0:4], axis=0, keepdims=True) * gain_row) * inv_count
    second_mean = group_sum(jnp.sum(summed[4:8], axis=0, keepdims=True) * gain_row) * inv_count
    factor = 1.0 / math.sqrt(POSITIONS)
    small_out[...] = jnp.concatenate(
        [
            whole[8:9],
            jnp.sum(whole[4:8], axis=0, keepdims=True),
            jnp.sum(whole[0:4], axis=0, keepdims=True),
            jnp.zeros((5, C), F32),
        ],
        axis=0,
    ) * factor

    def frame_grads(j, carry):
        at = pl.ds(pl.multiple_of(j * W, W), W)
        normed = (frames[0, j // RB, j % RB].astype(F32) - mean) * inverse_std
        result = inverse_std * (acc[at] * gain_row - first_mean - normed * second_mean)
        fg_out[0, j // RB, j % RB] = result.astype(BF16)
        return carry

    lax.fori_loop(0, FR * RB, frame_grads, 0)

    receive(qc.at[pl.ds(0, NZ - 1)], S_QC)
    push(qc, qd, S_QD, in_line((0, 1)))
    sent.append((qd, S_QD))
    receive(pc.at[pl.ds(0, PLANE - 1)], S_PC)
    push(pc, pd, S_PD, in_line((0, 1)))
    sent.append((pd, S_PD))
    write(pc, qc, c)
    receive(qd, S_QD)
    receive(pd, S_PD)
    write(pd, qd, 1 - c)
    finish()


def writer(enc, fg, wg, small, enc_out, fg_out, wg_out, bias_out, gain_out, shift_out, wide, sems):
    copies = [
        pltpu.make_async_copy(enc, enc_out, sems.at[0]),
        pltpu.make_async_copy(fg, fg_out, sems.at[1]),
    ]
    for copy in copies:
        copy.start()
    factor = 1.0 / math.sqrt(POSITIONS)
    part = TAP_ROWS // 3
    for k in range(3):
        at = pl.ds(k * part, part)
        wide[at] = wg[at].astype(F32) * factor
        copy = pltpu.make_async_copy(wide.at[at], wg_out.at[at], sems.at[2 + k])
        copy.start()
        copies.append(copy)
    bias_out[...] = small[0:1]
    gain_out[...] = small[1:2]
    shift_out[...] = small[2:3]
    for copy in copies:
        copy.wait()


def local(frames, cotangent, conv_weight, conv_bias, norm_gain, norm_shift, clip_ids):
    vmem = pl.BlockSpec(memory_space=pltpu.VMEM)
    hbm = pl.BlockSpec(memory_space=pltpu.HBM)
    row = jax.ShapeDtypeStruct((1, C), F32)
    operands = (
        frames,
        cotangent,
        conv_weight.reshape(9, 3 * C, C),
        conv_bias.reshape(1, C),
        norm_gain.reshape(1, C),
        norm_shift.reshape(1, C),
        clip_ids,
    )
    enc, fg, wg, small = pl.pallas_call(
        kernel,
        out_shape=(
            jax.ShapeDtypeStruct(frames.shape, BF16),
            jax.ShapeDtypeStruct(frames.shape, BF16),
            jax.ShapeDtypeStruct((TAP_ROWS, C), BF16),
            jax.ShapeDtypeStruct((8, C), F32),
        ),
        in_specs=[hbm] * 7,
        out_specs=(vmem,) * 4,
        scratch_shapes=[
            pltpu.VMEM(frames.shape, BF16),
            pltpu.VMEM(frames.shape, BF16),
            pltpu.VMEM((9, 3 * C, C), BF16),
            pltpu.VMEM((1, C), F32),
            pltpu.VMEM((1, C), F32),
            pltpu.VMEM((1, C), F32),
            pltpu.SMEM((SPANS,), jnp.int32),
            pltpu.VMEM((FR + 2, RB + 2, W, C), BF16),
            pltpu.VMEM((FR + 2, RB + 2, W, C), BF16),
            pltpu.VMEM((FR + 2, RB + 2, W, C), BF16),
            pltpu.VMEM((FR + 2, 3 * C, RB * W), BF16),
            pltpu.VMEM((FR + 2, RB + 2, W, 3 * C), BF16),
            pltpu.VMEM((FR + 2, RB + 2, W, 3 * C), BF16),
            pltpu.VMEM((9, C, 3 * C), BF16),
            pltpu.VMEM((8, C), F32),
            pltpu.VMEM((PLANE, 8, C), F32),
            pltpu.VMEM((8, C), F32),
            pltpu.VMEM((LINE, 8, C), F32),
            pltpu.VMEM((8, C), F32),
            pltpu.VMEM((PLANE, 8, C), F32),
            pltpu.VMEM((16, C), F32),
            pltpu.VMEM((LINE, 16, C), F32),
            pltpu.VMEM((LINE, 8, C), F32),
            pltpu.VMEM((NC * REGION, C), BF16),
            pltpu.VMEM((NC * REGION, C), F32),
            pltpu.VMEM((REGION, C), BF16),
            pltpu.VMEM((REGION, C), BF16),
            pltpu.VMEM((PLANE, CHUNK_P, C), BF16),
            pltpu.VMEM((NZ, CHUNK_P, C), BF16),
            pltpu.VMEM((PLANE, CHUNK_P, C), BF16),
            pltpu.VMEM((PLANE, CHUNK_P, C), BF16),
            pltpu.VMEM((NZ, CHUNK_Q, C), BF16),
            pltpu.VMEM((PLANE, CHUNK_Q, C), BF16),
            pltpu.VMEM((NZ, CHUNK_Q, C), BF16),
            pltpu.VMEM((NZ, CHUNK_Q, C), BF16),
            pltpu.VMEM((FR * RB * W, C), F32),
            pltpu.VMEM((FR * RB * W, C), F32),
            pltpu.SemaphoreType.DMA((SEMS,)),
            pltpu.SemaphoreType.DMA((SEMS,)),
            pltpu.SemaphoreType.DMA((7,)),
        ],
        compiler_params=pltpu.CompilerParams(
            collective_id=0, has_side_effects=True, vmem_limit_bytes=48 * 2**20
        ),
        cost_estimate=pl.CostEstimate(flops=3 * 10**9, bytes_accessed=4 * 10**6, transcendentals=10**6),
        name="block",
    )(*(pltpu.with_memory_space_constraint(v, pltpu.HBM) for v in operands))
    enc, fg, wg, bias, gain, shift = pl.pallas_call(
        writer,
        out_shape=(
            jax.ShapeDtypeStruct(frames.shape, BF16),
            jax.ShapeDtypeStruct(frames.shape, BF16),
            jax.ShapeDtypeStruct((TAP_ROWS, C), F32),
            row, row, row,
        ),
        in_specs=[vmem] * 4,
        out_specs=(hbm,) * 3 + (vmem,) * 3,
        scratch_shapes=[pltpu.VMEM((TAP_ROWS, C), F32), pltpu.SemaphoreType.DMA((5,))],
        compiler_params=pltpu.CompilerParams(vmem_limit_bytes=32 * 2**20),
        name="writer",
    )(enc, fg, wg, small)
    return (
        enc, fg, wg.reshape(conv_weight.shape),
        bias.reshape(C), gain.reshape(C), shift.reshape(C),
    )


def solution(mesh):
    placed = (P("span", None, "space", None, None),) * 2 + (P(),) * 5
    return jax.shard_map(
        local,
        mesh=mesh,
        in_specs=placed,
        out_specs=(P("span", None, "space", None, None),) * 2 + (P(),) * 4,
        check_vma=False,
    )
```
